512 devices in a mesh: wide: 64 (over x, z, core), narrow: 8 (over y).
Axes of the slice: x: 4, y: 8, z: 8, core: 2. Of those that a mesh axis runs over, the one named last changes fastest.
Arguments:
- core: float32 [512, 384, 384], P(('wide', 'narrow')), may hold values from -0.25371838 to 0.25371838
- next_core: float32 [384, 512, 384], P(None, ('wide', 'narrow')), may hold values from -37.5 to 37.5
- start_block: float32 [384, 192], replicated, may hold values from -6 to 6
Outputs:
- core_out: float32 [512, 384, 192], P(('wide', 'narrow'))
- next_out: float32 [192, 512, 384], P(None, ('wide', 'narrow'))
The draws below stay inside these ranges and needn't reach their ends.
All inputs are finite; a program needn't handle non-finite values.
Results may differ from the reference program's by a relative error of at most 0.0003.
Values sent between devices are 32-bit elements; how exact they have to be, the bound alone decides.
A program may use at most 64 MiB of HBM per device.

```python
import math
import jax
import jax.numpy as jnp
from jax import lax

RANK = 384
TRUNC = 192
ITERS = 6
MODES = 512


def draw_core(key, part):
    key = jax.random.fold_in(key, 11)
    keys = jax.random.split(key, 3)
    shape = (MODES, RANK, RANK)
    base = jnp.clip(jax.random.normal(keys[0], shape, jnp.float32), -5.0, 5.0)
    rising = jnp.exp(math.log(3.0) * jnp.arange(MODES, dtype=jnp.float32) / (MODES - 1)).reshape(MODES, 1, 1)
    row_scale = jnp.exp(math.log(10.0) * jax.random.uniform(keys[1], (MODES, RANK, 1), jnp.float32))
    col_scale = jnp.exp(math.log(3.0) * jax.random.uniform(keys[2], (1, 1, RANK), jnp.float32))
    return base * rising * row_scale * col_scale / (4.0 * math.sqrt(MODES * RANK))


def draw_next_core(key, part):
    key = jax.random.fold_in(key, 23)
    keys = jax.random.split(key, 2)
    shape = (RANK, MODES, RANK)
    base = jnp.clip(jax.random.normal(keys[0], shape, jnp.float32), -5.0, 5.0)
    rising = jnp.exp(math.log(3.0) * jnp.arange(MODES, dtype=jnp.float32) / (MODES - 1)).reshape(1, MODES, 1)
    col_scale = jnp.exp(math.log(10.0) * jax.random.uniform(keys[1], (1, MODES, RANK), jnp.float32))
    return base * rising * col_scale / 4.0


def scatter_about(key, shape, scale, reach, kind=jnp.bfloat16):
    return jnp.clip(scale * jax.random.normal(key, shape, jnp.float32), -reach, reach).astype(kind)


def setup_inputs(seed: int = 0) -> dict:
    arg_keys = jax.random.split(jax.random.key(seed), 4)
    return {
        "core": draw_core(jax.random.fold_in(arg_keys[3], 71), 0),
        "next_core": draw_next_core(jax.random.fold_in(arg_keys[3], 71), 0),
        "start_block": scatter_about(arg_keys[2], (RANK, TRUNC), 1.0, 6.0, jnp.float32),
    }


def orthonormal(block):
    square = jnp.dot(block.T.astype(jnp.float32), block.astype(jnp.float32), precision=lax.Precision.HIGHEST, preferred_element_type=jnp.float32)
    factor = jnp.linalg.cholesky(square)
    return jax.scipy.linalg.solve_triangular(factor, block.T, lower=True).T

def reference(core, next_core, start_block):
    highest = lax.Precision.HIGHEST
    flat_core = core.reshape(MODES * RANK, RANK)
    flat_next = next_core.reshape(RANK, MODES * RANK)
    gram = jnp.dot(flat_core.T.astype(jnp.float32), flat_core.astype(jnp.float32), precision=highest, preferred_element_type=jnp.float32)
    lower_factor = jnp.linalg.cholesky(gram)
    upper_factor = lower_factor.T
    ortho_t = jax.scipy.linalg.solve_triangular(lower_factor, flat_core.T, lower=True)
    moved = jnp.dot(upper_factor.astype(jnp.float32), flat_next.astype(jnp.float32), precision=highest, preferred_element_type=jnp.float32)
    cross = jnp.dot(flat_next.astype(jnp.float32), flat_next.T.astype(jnp.float32), precision=highest, preferred_element_type=jnp.float32)
    bond_gram = jnp.dot(jnp.dot(upper_factor.astype(jnp.float32), cross.astype(jnp.float32), precision=highest, preferred_element_type=jnp.float32).astype(jnp.float32), lower_factor.astype(jnp.float32), precision=highest, preferred_element_type=jnp.float32)
    basis = start_block
    for step in range(ITERS):
        basis = orthonormal(jnp.dot(bond_gram.astype(jnp.float32), basis.astype(jnp.float32), precision=highest, preferred_element_type=jnp.float32))
    scale = math.sqrt(MODES * RANK)
    core_out = scale * jnp.dot(ortho_t.T.astype(jnp.float32), basis.astype(jnp.float32), precision=highest, preferred_element_type=jnp.float32)
    next_out = jnp.dot(basis.T.astype(jnp.float32), moved.astype(jnp.float32), precision=highest, preferred_element_type=jnp.float32)
    return (core_out.reshape(MODES, RANK, TRUNC), next_out.reshape(TRUNC, MODES, RANK))
```

```python
import functools
import math

import jax
import jax.numpy as jnp
from jax import lax
from jax.experimental import pallas as pl
from jax.experimental.pallas import tpu as pltpu
from jax.sharding import PartitionSpec as P

RANK = 384
HI = lax.Precision.HIGHEST
NN = (((1,), (0,)), ((), ()))
NT = (((1,), (1,)), ((), ()))
TN = (((0,), (0,)), ((), ()))

def dot6(a, b, dims):
    return lax.dot_general(a, b, dims, precision=HI, preferred_element_type=jnp.float32)

def split(a):
    hi = a.astype(jnp.bfloat16)
    return hi, (a - hi.astype(jnp.float32)).astype(jnp.bfloat16)

def dot3(a, b, dims):
    ah, al = a if isinstance(a, tuple) else split(a)
    bh, bl = b if isinstance(b, tuple) else split(b)
    one = lambda x, y: lax.dot_general(x, y, dims, preferred_element_type=jnp.float32)
    return one(ah, bh) + (one(ah, bl) + one(al, bh))

def factor(mats, off):
    n = len(mats[0])
    sub = lax.broadcasted_iota(jnp.int32, (8, 128), 0)
    for t in range(n):
        for A in mats:
            P = A[t]
            c0 = off + 8 * t
            cb = [jnp.broadcast_to(P[:, c0+j:c0+j+1], (8, 128)) for j in range(8)]
            rows, rs, bs = [], [], {}
            dv = None
            for j in range(8):
                dj = jnp.broadcast_to(cb[j][j:j+1, :], (8, 128))
                r = 1.0 / dj
                rowj = jnp.broadcast_to(P[j:j+1, :], (8, 128))
                dv = dj if j == 0 else jnp.where(sub == j, dj, dv)
                rows.append(rowj); rs.append(r)
                m = jnp.where(sub > j, cb[j] * r, 0.0)
                P = P - m * rowj
                for i in range(j+1, 8):
                    b = jnp.broadcast_to(cb[j][i:i+1, :], (8, 128))
                    bs[(j, i)] = b
                    cb[i] = cb[i] - m * b
            A[t] = P * lax.rsqrt(dv)
            for u in range(t+1, n):
                X = A[u]
                cu = [jnp.broadcast_to(X[:, c0+j:c0+j+1], (8, 128)) for j in range(8)]
                for j in range(8):
                    m = cu[j] * rs[j]
                    X = X - m * rows[j]
                    for i in range(j+1, 8):
                        cu[i] = cu[i] - m * bs[(j, i)]
                A[u] = X
    return mats

def with_eye(s, off):
    row = lax.broadcasted_iota(jnp.int32, (64, 128), 0)
    col = lax.broadcasted_iota(jnp.int32, (64, 128), 1)
    eye = jnp.where(col == row + (64 - off), 1.0, 0.0)
    half = (col >= 64) if off else (col < 64)
    a = jnp.where(half, s, eye)
    return [a[8*t:8*t+8, :] for t in range(8)]

def inverses(mats, off):
    done = factor(mats, off)
    return [jnp.concatenate(m, axis=0)[:, 64 - off:128 - off] for m in done]

def body(scale, g_ref, m_ref, s_ref, c_ref, w_ref, co_ref, no_ref, r_ref, kh_ref, kl_ref, y_ref, p1_ref, p2_ref, f_ref, *a_refs):
    ds, dm, dg, dl = dot6, dot3, dot3, dot3
    for q in range(6):
        a_refs[q][...] = g_ref[64*q:64*q+64, :]
    r_ref[...] = jnp.zeros_like(r_ref)
    g = g_ref[...]
    k = ds(g, m_ref[...], NN)
    h = ds(k, g, NN)
    for x, lo in ((k, 0), (h, 384)):
        xh, xl = split(x)
        kh_ref[:, lo:lo+384] = xh
        kl_ref[:, lo:lo+384] = xl
    for p in range(6):
        o = 128 * (p // 2)
        off = 64 * (p % 2)
        (li,) = inverses([with_eye(a_refs[p][:, o:o+128], off)], off)
        rp = ds(li, a_refs[p][:, o:], NN)
        if off:
            col = lax.broadcasted_iota(jnp.int32, rp.shape, 1)
            rp = jnp.where(col >= 64, rp, 0.0)
        r_ref[64*p:64*p+64, o:] = rp
        if p < 5:
            for q in range(p+1, 6):
                oq = 128 * (q // 2)
                lq = rp[:, 64*q-o:64*q-o+64]
                a_refs[q][:, oq:] -= ds(lq, rp[:, oq-o:], TN)
    z0 = ds(ds(s_ref[...], r_ref[...], NN), m_ref[...], NN)
    y_ref[:, :384] = z0
    y_ref[:, 384:] = ds(z0, g_ref[...], NN)
    p1_ref[...] = jnp.zeros_like(p1_ref)
    p2_ref[...] = jnp.zeros_like(p2_ref)

    def wave(w, _):
        y = [y_ref[64*j:64*j+64, :] for j in range(3)]
        prev1, prev2 = p1_ref[...], p2_ref[...]
        z = [v[:, :384] for v in y]
        u = [v[:, 384:] for v in y]
        ss, cs = [], [None]
        s0 = dg(u[0], jnp.concatenate([prev1[:, :384], z[0]], axis=0), NT)
        e1 = dg(u[1], jnp.concatenate([prev1[:, :384], z[1]], axis=0), NT)
        e2 = dg(u[2], prev2[:, :384], NT)
        s2 = dg(u[2], jnp.concatenate([prev1[:, :384], z[2]], axis=0), NT)
        c1 = e1[:, :64]
        c1w = jnp.concatenate([c1, c1], axis=0)
        s1 = e1 - dg(c1, c1w, NT)
        e2w = jnp.concatenate([e2, e2], axis=0)
        s2 = s2 - dg(e2, e2w, NT)
        li = inverses([with_eye(s, 64) for s in (s0, s1, s2)], 64)
        x = [y[0], y[1] - dg(c1, prev1, NN), y[2] - dg(e2, prev2, NN)]
        n = [dl(li[j], x[j], NN) for j in range(3)]
        p2_ref[0:64, :] = prev1
        p2_ref[64:128, :] = n[1]
        p1_ref[...] = n[0]
        for j in range(3):
            @pl.when(w - j < 6)
            def _(j=j):
                f_ref[64*j:64*j+64, :] = n[j]
        nz = jnp.concatenate([v[:, :384] for v in n], axis=0)
        ny = dm(nz, (kh_ref[...], kl_ref[...]), NN)
        for j in range(3):
            @pl.when(w >= j)
            def _(j=j):
                y_ref[64*j:64*j+64, :] = ny[64*j:64*j+64, :]
        return 0

    lax.fori_loop(0, 8, wave, 0)
    co_ref[...] = scale * dot3(f_ref[:, :384], c_ref[0], NT)
    no_ref[:, 0, :] = dot3(f_ref[:, 384:], w_ref[:, 0, :], NN)

def finish(g, m, st, core, nxt, scale):
    v = pl.BlockSpec(memory_space=pltpu.VMEM)
    return pl.pallas_call(
        functools.partial(body, scale),
        out_shape=(jax.ShapeDtypeStruct((192, 384), jnp.float32), jax.ShapeDtypeStruct((192, 1, 384), jnp.float32)),
        in_specs=[v] * 5, out_specs=(v, v),
        scratch_shapes=[pltpu.VMEM((384, 384), jnp.float32), pltpu.VMEM((384, 768), jnp.bfloat16), pltpu.VMEM((384, 768), jnp.bfloat16),
            pltpu.VMEM((192, 768), jnp.float32), pltpu.VMEM((64, 768), jnp.float32), pltpu.VMEM((128, 768), jnp.float32),
            pltpu.VMEM((192, 768), jnp.float32)] + [pltpu.VMEM((64, 384), jnp.float32)] * 6,
        compiler_params=pltpu.CompilerParams(vmem_limit_bytes=48 * 1024 * 1024),
    )(g, m, st, core, nxt)


MESH = pl.DeviceIdType.MESH
PAIRS = ((0, 0), (0, 1), (0, 2), (1, 1), (1, 2), (2, 2))


def reduce_body(core_ref, next_ref, g_ref, m_ref, acc, r1, s1, r2, s2, r3, r4, res, send_sem, recv_sem):
    wide, y = lax.axis_index("wide"), lax.axis_index("narrow")
    core, z, x = lax.rem(wide, 2), lax.rem(wide // 2, 8), wide // 16

    def place(x, y, z, core):
        return ((x * 8 + z) * 2 + core, y)

    sibling = place(x, y, z, 1 - core)
    along_x = [place(lax.rem(x + d, 4), y, z, core) for d in range(1, 4)]
    along_y = [place(x, lax.rem(y + d, 8), z, core) for d in range(1, 8)]
    along_z = [place(x, y, lax.rem(z + d, 8), core) for d in range(1, 8)]

    barrier = pltpu.get_barrier_semaphore()
    for other in [sibling] + along_x + along_y + along_z:
        pl.semaphore_signal(barrier, inc=1, device_id=other, device_id_type=MESH)

    c = split(core_ref[0])
    w = split(next_ref[:, 0, :])
    gram = dot3(c, c, TN)
    cross = dot3(w, w, NT)
    for b, (i, j) in enumerate(PAIRS):
        for k, a in ((0, gram), (6, cross)):
            block = a[128*i:128*i+128, 128*j:128*j+128]
            acc[16*(b+k):16*(b+k)+16] = block.reshape(16, 8, 128)
    pl.semaphore_wait(barrier, 18)

    count = [0]

    def copy(src, dst, other):
        n = count[0]
        count[0] += 1
        d = pltpu.make_async_remote_copy(src_ref=src, dst_ref=dst, send_sem=send_sem.at[n], recv_sem=recv_sem.at[n],
                                         device_id=other, device_id_type=MESH)
        d.start()
        return d

    sent = [copy(acc.at[pl.ds(96 * (1 - core), 96)], r1, sibling)]
    sent[0].wait_recv()
    s1[...] = acc[pl.ds(96 * core, 96)] + r1[...]

    step = [copy(s1.at[pl.ds(24 * lax.rem(x + d, 4), 24)], r2.at[d-1], along_x[d-1]) for d in (2, 1, 3)]
    for d in step:
        d.wait_recv()
    sent += step
    s2[...] = s1[pl.ds(24 * x, 24)] + r2[0] + (r2[1] + r2[2])

    step = [copy(s2.at[pl.ds(3 * lax.rem(y + d, 8), 3)], r3.at[d-1], along_y[d-1]) for d in (4, 3, 5, 2, 6, 1, 7)]
    for d in step:
        d.wait_recv()
    sent += step
    total = s2[pl.ds(3 * y, 3)]
    for d in range(7):
        total = total + r3[d]
    r4[z] = total

    step = [copy(r4.at[z], r4.at[z], along_z[d-1]) for d in (4, 3, 5, 2, 6, 1, 7)]
    for d in step:
        d.wait_recv()
    sent += step
    total = r4[0]
    for d in range(1, 8):
        total = total + r4[d]
    at = 96 * core + 24 * x + 3 * y
    res[pl.ds(at, 3)] = total

    mine = res.at[pl.ds(at, 3)]
    step = [copy(mine, mine, along_y[d-1]) for d in (4, 3, 5, 2, 6, 1, 7)]
    for d in step:
        d.wait_recv()
    sent += step
    mine = res.at[pl.ds(96 * core + 24 * x, 24)]
    step = [copy(mine, mine, along_x[d-1]) for d in (2, 1, 3)]
    for d in step:
        d.wait_recv()
    sent += step
    mine = res.at[pl.ds(96 * core, 96)]
    step = [copy(mine, mine, sibling)]
    step[0].wait_recv()
    sent += step
    for b, (i, j) in enumerate(PAIRS):
        for k, out in ((0, g_ref), (6, m_ref)):
            block = res[16*(b+k):16*(b+k)+16].reshape(128, 128)
            out[128*i:128*i+128, 128*j:128*j+128] = block
            if i < j:
                out[128*j:128*j+128, 128*i:128*i+128] = block.T
    for d in sent:
        d.wait_send()


def reduced(core, nxt):
    v = pl.BlockSpec(memory_space=pltpu.VMEM)
    tile = lambda *lead: pltpu.VMEM(lead + (8, 128), jnp.float32)
    square = jax.ShapeDtypeStruct((RANK, RANK), jnp.float32)
    return pl.pallas_call(
        reduce_body,
        out_shape=(square, square),
        in_specs=[v, v], out_specs=(v, v),
        scratch_shapes=[tile(192), tile(96), tile(96), tile(3, 24), tile(24), tile(7, 3), tile(8, 3), tile(192),
                        pltpu.SemaphoreType.DMA((29,)), pltpu.SemaphoreType.DMA((29,))],
        compiler_params=pltpu.CompilerParams(collective_id=0, has_side_effects=True, vmem_limit_bytes=48 * 1024 * 1024),
    )(core, nxt)


def shards(core, next_core, start_block):
    gram, cross = reduced(core, next_core)
    scale = math.sqrt(core.shape[0] * lax.axis_size("wide") * lax.axis_size("narrow") * core.shape[1])
    core_t, next_out = finish(gram, cross, start_block.T, core, next_core, scale)
    return core_t.T[None], next_out


def solution(mesh):
    placed = (P(("wide", "narrow"), None, None), P(None, ("wide", "narrow"), None), P())
    return jax.shard_map(
        shards,
        mesh=mesh,
        in_specs=placed,
        out_specs=(P(("wide", "narrow"), None, None), P(None, ("wide", "narrow"), None)),
        check_vma=False,
    )
```

```python
import functools
import math

import jax
import jax.numpy as jnp
from jax import lax
from jax.experimental import pallas as pl
from jax.experimental.pallas import tpu as pltpu
from jax.sharding import PartitionSpec as P

RANK = 384
ITERS = 6
MESH = pl.DeviceIdType.MESH
PAIRS = ((0, 0), (0, 1), (0, 2), (1, 1), (1, 2), (2, 2))
HI = lax.Precision.HIGHEST
NN = (((1,), (0,)), ((), ()))
NT = (((1,), (1,)), ((), ()))
TN = (((0,), (0,)), ((), ()))


def dot6(a, b, dims):
    return lax.dot_general(a, b, dims, precision=HI, preferred_element_type=jnp.float32)


def split(a):
    hi = a.astype(jnp.bfloat16)
    return hi, (a - hi.astype(jnp.float32)).astype(jnp.bfloat16)


def dot3(a, b, dims):
    ah, al = a if isinstance(a, tuple) else split(a)
    bh, bl = b if isinstance(b, tuple) else split(b)
    one = lambda x, y: lax.dot_general(x, y, dims, preferred_element_type=jnp.float32)
    if dims == TN:
        return one(ah, bh) + (one(ah, bl) + one(al, bh))
    rows = ah.shape[0]
    both = one(jnp.concatenate([ah, al], axis=0), bh)
    return both[:rows] + (both[rows:] + one(ah, bl))


def row_of(v, j):
    return jnp.broadcast_to(v[j:j+1, :], (8, 128))


def factor(groups, gj):
    sub = lax.broadcasted_iota(jnp.int32, (8, 128), 0)
    lane_id = lax.broadcasted_iota(jnp.int32, (8, 128), 1)
    n = 8

    def lanes(pair, X, t):
        if not pair:
            return [jnp.broadcast_to(X[:, 64+8*t+j:64+8*t+j+1], (8, 128)) for j in range(8)]
        base = jnp.where(lane_id < 64, 0, 64)
        return [jnp.take_along_axis(X, base + (8*t + j), axis=1) for j in range(8)]

    ahead = [lanes(pair, tiles[0][0], 0) for pair, tiles in groups]
    for t in range(n):
        for g, (pair, A) in enumerate(groups):
            cb = ahead[g]
            P = A[t]
            W = list(P)
            dv = rv = None
            last = t + 1 == n
            if not last:
                X = A[t+1]
                cu = lanes(pair, X[0], t)
                cn = lanes(pair, X[0], t+1)
            others = range(t+2, n)
            if not gj:
                co = {u: lanes(pair, A[u][0], t) for u in others}
            for j in range(8):
                dj = row_of(cb[j], j)
                r = 1.0 / dj
                dv = dj if j == 0 else jnp.where(sub == j, dj, dv)
                rows = [row_of(p, j) for p in P]
                bs = {i: row_of(cb[j], i) for i in range(j+1, 8)}
                if gj:
                    rv = r if j == 0 else jnp.where(sub == j, r, rv)
                    mg = jnp.where(sub == j, 0.0, cb[j] * r)
                    W = [w - mg * x for w, x in zip(W, rows)]
                    mf = jnp.where(sub > j, mg, 0.0)
                else:
                    mg = mf = jnp.where(sub > j, cb[j] * r, 0.0)
                P = [p - mf * x for p, x in zip(P, rows)]
                for i in range(j+1, 8):
                    cb[i] = cb[i] - mg * bs[i]
                if not last:
                    m = cu[j] * r
                    X = [a - m * x for a, x in zip(X, rows)]
                    for i in range(8):
                        cn[i] = cn[i] - m * row_of(cu[j], i)
                    for i in range(j+1, 8):
                        cu[i] = cu[i] - m * bs[i]
                if not gj:
                    for u in others:
                        m = co[u][j] * r
                        A[u] = [a - m * x for a, x in zip(A[u], rows)]
                        for i in range(j+1, 8):
                            co[u][i] = co[u][i] - m * bs[i]
            s = lax.rsqrt(dv)
            A[t] = [p * s for p in P]
            if not last:
                A[t+1] = X
                ahead[g] = cn
            if gj and t + 2 < n:
                wr = [[row_of(w * rv, j) for j in range(8)] for w in W]
                for u in others:
                    co = lanes(pair, A[u][0], t)
                    new = []
                    for a, wv in zip(A[u], wr):
                        p = [co[j] * wv[j] for j in range(8)]
                        new.append(a - (((p[0] + p[1]) + (p[2] + p[3])) + ((p[4] + p[5]) + (p[6] + p[7]))))
                    A[u] = new
    return groups


def iotas(rows):
    return lax.broadcasted_iota(jnp.int32, (rows, 128), 0), lax.broadcasted_iota(jnp.int32, (rows, 128), 1)


def single(s):
    row, col = iotas(64)
    a = jnp.where(col >= 64, s, jnp.where(col == row, 1.0, 0.0))
    return False, [[a[8*t:8*t+8, :]] for t in range(8)]


def pair(s):
    row, col = iotas(64)
    eye = jnp.where((col == row) | (col == row + 64), 1.0, 0.0)
    return True, [[s[8*t:8*t+8, :], eye[8*t:8*t+8, :]] for t in range(8)]


def inverse(group):
    is_pair, tiles = group
    a = jnp.concatenate([t[-1] for t in tiles], axis=0)
    if not is_pair:
        return a[:, :64]
    row, col = iotas(128)
    return jnp.where((row < 64) == (col < 64), jnp.concatenate([a, a], axis=0), 0.0)


def sum_and_factor(core_hbm, next_hbm, r_ref, m_ref, ortho_ref, moved_ref, c_ref, w_ref, acc, r1, s1, r2, r4, res, *more):
    a_refs, t_refs = more[:6], more[6:12]
    in_sem, pair_send, pair_recv, plane_send, plane_recv, line_send, line_recv = more[12:]
    wide, y = lax.axis_index("wide"), lax.axis_index("narrow")
    core, z, x = lax.rem(wide, 2), lax.rem(wide // 2, 8), wide // 16

    def place(x, y, z, core):
        return ((x * 8 + z) * 2 + core, y)

    def in_plane(d):
        return lax.rem(x + d // 8, 4), lax.rem(z + lax.rem(d, 8), 8)

    sibling = place(x, y, z, 1 - core)
    along_y = [place(x, lax.rem(y + d, 8), z, core) for d in range(1, 8)]

    load_c = pltpu.make_async_copy(core_hbm, c_ref, in_sem.at[0])
    load_c.start()
    load_w = pltpu.make_async_copy(next_hbm, w_ref, in_sem.at[1])
    load_w.start()

    barrier = pltpu.get_barrier_semaphore()
    for other in [sibling] + along_y:
        pl.semaphore_signal(barrier, inc=1, device_id=other, device_id_type=MESH)

    def greet(d, _):
        px, pz = in_plane(d)
        pl.semaphore_signal(barrier, inc=1, device_id=place(px, y, pz, core), device_id_type=MESH)
        return 0

    lax.fori_loop(1, 32, greet, 0)

    def remote(src, dst, send, recv, other):
        return pltpu.make_async_remote_copy(src_ref=src, dst_ref=dst, send_sem=send, recv_sem=recv, device_id=other, device_id_type=MESH)

    def fill(k, a):
        for b, (i, j) in enumerate(PAIRS):
            acc[k, 32*b:32*b+32] = a[128*i:128*i+128, 128*j:128*j+128].reshape(32, 4, 128)

    def pair_out(k):
        return remote(acc.at[k, pl.ds(96 * (1 - core), 96)], r1.at[k], pair_send.at[0, k], pair_recv.at[0, k], sibling)

    def pair_back(k):
        mine = res.at[k, pl.ds(96 * core, 96)]
        return remote(mine, mine, pair_send.at[1, k], pair_recv.at[1, k], sibling)

    def plane_out(k, d):
        px, pz = in_plane(d)
        return remote(s1.at[k, pl.ds(3 * (px * 8 + pz), 3)], r2.at[k, d - 1], plane_send.at[0, k, d - 1], plane_recv.at[0, k, d - 1],
                      place(px, y, pz, core))

    at = 96 * core + 3 * (x * 8 + z)

    def plane_back(k, d):
        px, pz = in_plane(d)
        mine = res.at[k, pl.ds(at, 3)]
        return remote(mine, mine, plane_send.at[1, k, d - 1], plane_recv.at[1, k, d - 1], place(px, y, pz, core))

    def line(k, d):
        return remote(r4.at[k, y], r4.at[k, y], line_send.at[k, d - 1], line_recv.at[k, d - 1], along_y[d - 1])

    def each(what):
        def step(d, _):
            what(d)
            return 0

        lax.fori_loop(1, 32, step, 0)

    def pair_sum(k):
        pair_out(k).wait_recv()
        s1[k] = acc[k, pl.ds(96 * core, 96)] + r1[k]
        each(lambda d: plane_out(k, d).start())

    def plane_sum(k):
        each(lambda d: plane_out(k, d).wait_recv())
        total = s1[k, pl.ds(3 * (x * 8 + z), 3)]
        parts = [r2[k, d] for d in range(31)]
        while len(parts) > 1:
            parts = [a + b for a, b in zip(parts[::2], parts[1::2])] + ([parts[-1]] if len(parts) % 2 else [])
        r4[k, y] = total + parts[0]
        for d in (4, 3, 5, 2, 6, 1, 7):
            line(k, d).start()

    def line_sum(k):
        for d in range(1, 8):
            line(k, d).wait_recv()
        p = [r4[k, d] for d in range(8)]
        res[k, pl.ds(at, 3)] = ((p[0] + p[1]) + (p[2] + p[3])) + ((p[4] + p[5]) + (p[6] + p[7]))
        each(lambda d: plane_back(k, d).start())

    def gathered(k):
        each(lambda d: plane_back(k, d).wait_recv())
        pair_back(k).start()

    load_c.wait()
    c = split(c_ref[0])
    fill(0, dot3(c, c, TN))
    pl.semaphore_wait(barrier, 39)
    pair_out(0).start()
    load_w.wait()
    w = split(w_ref[:, 0, :])
    fill(1, dot3(w, w, NT))
    pair_out(1).start()
    pair_sum(0)
    turned = c_ref[0].T
    for q in range(6):
        t_refs[q][...] = turned[64*q:64*q+64, :]
    r_ref[...] = jnp.zeros_like(r_ref)
    pair_sum(1)
    plane_sum(0)
    plane_sum(1)
    line_sum(0)
    line_sum(1)
    gathered(0)
    pair_back(0).wait_recv()

    def block(k, b):
        return res[k, 32*b:32*b+32].reshape(128, 128)

    for b, (i, j) in enumerate(PAIRS):
        a = block(0, b)
        a_refs[2*i][:, 128*j:128*j+128] = a[:64]
        a_refs[2*i+1][:, 128*j:128*j+128] = a[64:]
    for p in range(6):
        o = 128 * (p // 2)
        d = a_refs[p][:, o:o+128]
        if p % 2 == 0:
            d = pltpu.roll(d, 64, 1)
        (g,) = factor([single(d)], False)
        li = inverse(g)
        rp = dot6(li, a_refs[p][:, o:], NN)
        if p % 2:
            rp = jnp.where(lax.broadcasted_iota(jnp.int32, rp.shape, 1) >= 64, rp, 0.0)
        r_ref[64*p:64*p+64, o:] = rp
        ortho = dot3(li, t_refs[p][...], NN)
        ortho_ref[64*p:64*p+64, :] = ortho
        for q in range(p + 1, 6):
            oq = 128 * (q // 2)
            lq = rp[:, 64*q-o:64*q-o+64]
            a_refs[q][:, oq:] -= dot6(lq, rp[:, oq-o:], TN)
            t_refs[q][...] -= dot3(lq, ortho, TN)
        moved_ref[64*p:64*p+64, :] = dot3(rp, (w[0][o:, :], w[1][o:, :]), NN)
        if p == 1:
            gathered(1)
    pair_back(1).wait_recv()
    for b, (i, j) in enumerate(PAIRS):
        a = block(1, b)
        m_ref[128*i:128*i+128, 128*j:128*j+128] = a
        if i < j:
            m_ref[128*j:128*j+128, 128*i:128*i+128] = a.T
    for k in range(2):
        pair_out(k).wait_send()
        each(lambda d: plane_out(k, d).wait_send())
        for d in range(1, 8):
            line(k, d).wait_send()
        each(lambda d: plane_back(k, d).wait_send())
        pair_back(k).wait_send()


def first(core, nxt):
    v = pl.BlockSpec(memory_space=pltpu.VMEM)
    anywhere = pl.BlockSpec(memory_space=pl.ANY)
    f32 = lambda *s: pltpu.VMEM(s, jnp.float32)
    half = lambda *lead: pltpu.VMEM(lead + (4, 128), jnp.float32)
    sems = pltpu.SemaphoreType.DMA
    square = jax.ShapeDtypeStruct((RANK, RANK), jnp.float32)
    return pl.pallas_call(
        sum_and_factor,
        out_shape=(square,) * 4,
        in_specs=[anywhere] * 2, out_specs=(v,) * 4,
        scratch_shapes=[f32(1, RANK, RANK), f32(RANK, 1, RANK), half(2, 192), half(2, 96), half(2, 96), half(2, 31, 3), half(2, 8, 3), half(2, 192)]
        + [f32(64, RANK)] * 12
        + [sems((2,)), sems((2, 2)), sems((2, 2)), sems((2, 2, 31)), sems((2, 2, 31)), sems((2, 7)), sems((2, 7))],
        compiler_params=pltpu.CompilerParams(collective_id=0, has_side_effects=True, vmem_limit_bytes=40 * 1024 * 1024),
    )(core, nxt)


def iterate(scale, r_ref, m_ref, ortho_ref, moved_ref, s_ref, co_ref, no_ref, bh_ref, bl_ref, y_ref, p1_ref, p2_ref, f_ref):
    r = r_ref[...]
    rm = dot6(r, m_ref[...], NN)
    y_ref[...] = dot6(dot6(s_ref[...], rm, NN), r, NT)
    bh_ref[...], bl_ref[...] = split(dot6(rm, r, NT))
    p1_ref[...] = jnp.zeros_like(p1_ref)
    p2_ref[...] = jnp.zeros_like(p2_ref)

    def wave(w, _):
        y = [y_ref[64*j:64*j+64, :] for j in range(3)]
        ys = [split(v) for v in y]
        prev1, prev2 = p1_ref[...], p2_ref[...]
        p1s, p2s = split(prev1), split(prev2)
        stack = lambda *parts: tuple(jnp.concatenate([q[i] for q in parts], axis=0) for i in range(2))
        left = lambda q: (q[0][:, :RANK], q[1][:, :RANK])
        e0 = dot3(ys[0], stack(ys[0], ys[1]), NT)
        e1 = dot3(ys[1], stack(left(p1s), ys[1]), NT)
        e2 = dot3(ys[2], stack(left(p2s), ys[2], ys[2]), NT)
        c1, c2 = split(e1[:, :64]), split(e2[:, :128])
        s1 = e1 - dot3(c1, stack(c1, c1), NT)
        s2 = e2[:, 128:] - dot3(c2, stack(c2, c2), NT)
        col = lax.broadcasted_iota(jnp.int32, (64, 128), 1)
        g01, g2 = factor([pair(jnp.where(col < 64, e0, s1)), single(s2)], True)
        image = dot3(stack(*ys), (bh_ref[...], bl_ref[...]), NN)
        both = [jnp.concatenate([y[j], image[64*j:64*j+64]], axis=1) for j in range(3)]
        x1 = both[1] - dot3(c1, p1s, NN)
        x2 = both[2] - dot3(c2, p2s, NN)
        n01 = dot3(inverse(g01), jnp.concatenate([both[0], x1], axis=0), NN)
        n2 = dot3(inverse(g2), x2, NN)
        n = [n01[:64], n01[64:], n2]
        p2_ref[0:64, :] = prev1
        p2_ref[64:128, :] = n[1]
        p1_ref[...] = n[0]
        for j in range(3):
            @pl.when(w - j < ITERS)
            def _(j=j):
                f_ref[64*j:64*j+64, :] = n[j][:, :RANK]

            @pl.when(w >= j)
            def _(j=j):
                y_ref[64*j:64*j+64, :] = n[j][:, RANK:]
        return 0

    lax.fori_loop(0, ITERS + 2, wave, 0)
    f = split(f_ref[...])
    co_ref[...] = scale * dot3(f, ortho_ref[...], NN)
    no_ref[:, 0, :] = dot3(f, moved_ref[...], NN)


def second(r, m, ortho, moved, start, scale):
    v = pl.BlockSpec(memory_space=pltpu.VMEM)
    f32 = lambda *s: pltpu.VMEM(s, jnp.float32)
    bf16 = lambda *s: pltpu.VMEM(s, jnp.bfloat16)
    return pl.pallas_call(
        functools.partial(iterate, scale),
        out_shape=(jax.ShapeDtypeStruct((192, RANK), jnp.float32), jax.ShapeDtypeStruct((192, 1, RANK), jnp.float32)),
        in_specs=[v] * 5, out_specs=(v, v),
        scratch_shapes=[bf16(RANK, RANK), bf16(RANK, RANK), f32(192, RANK), f32(64, 2 * RANK), f32(128, 2 * RANK), f32(192, RANK)],
        compiler_params=pltpu.CompilerParams(vmem_limit_bytes=40 * 1024 * 1024),
    )(r, m, ortho, moved, start)


def shards(core, next_core, start_block):
    r, m, ortho, moved = first(core, next_core)
    scale = math.sqrt(core.shape[0] * lax.axis_size("wide") * lax.axis_size("narrow") * core.shape[1])
    core_t, next_out = second(r, m, ortho, moved, start_block.T, scale)
    return core_t.T[None], next_out


def solution(mesh):
    placed = (P(("wide", "narrow"), None, None), P(None, ("wide", "narrow"), None), P())
    return jax.shard_map(
        shards,
        mesh=mesh,
        in_specs=placed,
        out_specs=(P(("wide", "narrow"), None, None), P(None, ("wide", "narrow"), None)),
        check_vma=False,
    )
```

```python
import functools
import math

import jax
import jax.numpy as jnp
from jax import lax
from jax.experimental import pallas as pl
from jax.experimental.pallas import tpu as pltpu
from jax.sharding import PartitionSpec as P

RANK = 384
ITERS = 6
MESH = pl.DeviceIdType.MESH
PAIRS = ((0, 0), (0, 1), (0, 2), (1, 1), (1, 2), (2, 2))
HI = lax.Precision.HIGHEST
NN = (((1,), (0,)), ((), ()))
NT = (((1,), (1,)), ((), ()))
TN = (((0,), (0,)), ((), ()))


def dot6(a, b, dims):
    return lax.dot_general(a, b, dims, precision=HI, preferred_element_type=jnp.float32)


def split(a):
    hi = a.astype(jnp.bfloat16)
    return hi, (a - hi.astype(jnp.float32)).astype(jnp.bfloat16)


def dot3(a, b, dims):
    ah, al = a if isinstance(a, tuple) else split(a)
    bh, bl = b if isinstance(b, tuple) else split(b)
    one = lambda x, y: lax.dot_general(x, y, dims, preferred_element_type=jnp.float32)
    if dims == TN:
        return one(ah, bh) + (one(ah, bl) + one(al, bh))
    rows = ah.shape[0]
    both = one(jnp.concatenate([ah, al], axis=0), bh)
    return both[:rows] + (both[rows:] + one(ah, bl))


def row_of(v, j):
    return jnp.broadcast_to(v[j:j+1, :], (8, 128))


def factor(groups, gj):
    sub = lax.broadcasted_iota(jnp.int32, (8, 128), 0)
    lane_id = lax.broadcasted_iota(jnp.int32, (8, 128), 1)
    n = len(groups[0][1])

    def lanes(pair, X, t):
        if not pair:
            return [jnp.broadcast_to(X[:, 64+8*t+j:64+8*t+j+1], (8, 128)) for j in range(8)]
        base = jnp.where(lane_id < 64, 0, 64)
        return [jnp.take_along_axis(X, base + (8*t + j), axis=1) for j in range(8)]

    ahead = [lanes(pair, tiles[0][0], 0) for pair, tiles in groups]
    for t in range(n):
        for g, (pair, A) in enumerate(groups):
            cb = ahead[g]
            P = A[t]
            W = list(P)
            dv = rv = None
            last = t + 1 == n
            if not last:
                X = A[t+1]
                cu = lanes(pair, X[0], t)
                cn = lanes(pair, X[0], t+1)
            others = range(t+2, n)
            if not gj:
                co = {u: lanes(pair, A[u][0], t) for u in others}
            for j in range(8):
                dj = row_of(cb[j], j)
                r = 1.0 / dj
                dv = dj if j == 0 else jnp.where(sub == j, dj, dv)
                rows = [row_of(p, j) for p in P]
                bs = {i: row_of(cb[j], i) for i in range(j+1, 8)}
                if gj:
                    rv = r if j == 0 else jnp.where(sub == j, r, rv)
                    mg = jnp.where(sub == j, 0.0, cb[j] * r)
                    W = [w - mg * x for w, x in zip(W, rows)]
                    mf = jnp.where(sub > j, mg, 0.0)
                else:
                    mg = mf = jnp.where(sub > j, cb[j] * r, 0.0)
                P = [p - mf * x for p, x in zip(P, rows)]
                for i in range(j+1, 8):
                    cb[i] = cb[i] - mg * bs[i]
                if not last:
                    m = cu[j] * r
                    X = [a - m * x for a, x in zip(X, rows)]
                    for i in range(8):
                        cn[i] = cn[i] - m * row_of(cu[j], i)
                    for i in range(j+1, 8):
                        cu[i] = cu[i] - m * bs[i]
                if not gj:
                    for u in others:
                        m = co[u][j] * r
                        A[u] = [a - m * x for a, x in zip(A[u], rows)]
                        for i in range(j+1, 8):
                            co[u][i] = co[u][i] - m * bs[i]
            s = lax.rsqrt(dv)
            A[t] = [p * s for p in P]
            if not last:
                A[t+1] = X
                ahead[g] = cn
            if gj and t + 2 < n:
                wr = [[row_of(w * rv, j) for j in range(8)] for w in W]
                for u in others:
                    co = lanes(pair, A[u][0], t)
                    new = []
                    for a, wv in zip(A[u], wr):
                        p = [co[j] * wv[j] for j in range(8)]
                        new.append(a - (((p[0] + p[1]) + (p[2] + p[3])) + ((p[4] + p[5]) + (p[6] + p[7]))))
                    A[u] = new
    return groups


def iotas(rows):
    return lax.broadcasted_iota(jnp.int32, (rows, 128), 0), lax.broadcasted_iota(jnp.int32, (rows, 128), 1)


def single(s):
    row, col = iotas(64)
    a = jnp.where(col >= 64, s, jnp.where(col == row, 1.0, 0.0))
    return False, [[a[8*t:8*t+8, :]] for t in range(8)]


def pair(s):
    row, col = iotas(s.shape[0])
    eye = jnp.where((col == row) | (col == row + 64), 1.0, 0.0)
    return True, [[s[8*t:8*t+8, :], eye[8*t:8*t+8, :]] for t in range(s.shape[0] // 8)]


def inverse(group):
    is_pair, tiles = group
    a = jnp.concatenate([t[-1] for t in tiles], axis=0)
    if not is_pair:
        return a[:, :64]
    if a.shape[0] < 64:
        a = jnp.concatenate([a, jnp.zeros((64 - a.shape[0], 128), jnp.float32)], axis=0)
    row, col = iotas(128)
    return jnp.where((row < 64) == (col < 64), jnp.concatenate([a, a], axis=0), 0.0)


def sum_and_factor(c_ref, w_ref, r_ref, m_ref, ortho_ref, moved_ref, acc, r1, s1, r2, r4, res, *more):
    a_refs, t_refs = more[:6], more[6:12]
    pair_send, pair_recv, plane_send, plane_recv, row_recv, line_send, line_recv = more[12:]
    wide, y = lax.axis_index("wide"), lax.axis_index("narrow")
    core, z, x = lax.rem(wide, 2), lax.rem(wide // 2, 8), wide // 16

    def place(x, y, z, core):
        return ((x * 8 + z) * 2 + core, y)

    def in_plane(d):
        return lax.rem(x + d // 8, 4), lax.rem(z + lax.rem(d, 8), 8)

    sibling = place(x, y, z, 1 - core)
    along_y = [place(x, lax.rem(y + d, 8), z, core) for d in range(1, 8)]

    barrier = pltpu.get_barrier_semaphore()
    for other in [sibling] + along_y:
        pl.semaphore_signal(barrier, inc=1, device_id=other, device_id_type=MESH)

    def greet(d, _):
        px, pz = in_plane(d)
        pl.semaphore_signal(barrier, inc=1, device_id=place(px, y, pz, core), device_id_type=MESH)
        return 0

    lax.fori_loop(1, 32, greet, 0)

    def remote(src, dst, send, recv, other):
        return pltpu.make_async_remote_copy(src_ref=src, dst_ref=dst, send_sem=send, recv_sem=recv, device_id=other, device_id_type=MESH)

    def fill(k, a):
        for b, (i, j) in enumerate(PAIRS):
            acc[k, 32*b:32*b+32] = a[128*i:128*i+128, 128*j:128*j+128].reshape(32, 4, 128)

    def whole(ref, send, recv):
        return remote(ref, ref, send, recv, sibling)

    def pair_out(k):
        return remote(acc.at[k, pl.ds(96 * (1 - core), 96)], r1.at[k], pair_send.at[k, 4], pair_recv.at[k, 4], sibling)

    at = 96 * core + 3 * (x * 8 + z)

    def plane_copies(make):
        for dx in (2, 1, 3, 0):
            def step(i, _, dx=dx):
                dz = 1 + lax.rem(2 + i, 7) if dx == 0 else lax.rem(4 + i, 8)
                make(dx, dz, lax.rem(x + dx, 4), lax.rem(z + dz, 8))
                return 0

            lax.fori_loop(1 if dx == 0 else 0, 8, step, 0, unroll=True)

    def plane_out(k):
        def make(dx, dz, px, pz):
            remote(s1.at[k, pl.ds(3 * (px * 8 + pz), 3)], r2.at[k, dx * 8 + dz - 1], plane_send.at[0, k], plane_recv.at[k],
                   place(px, y, pz, core)).start()

        plane_copies(make)

    def plane_back(k):
        mine = res.at[k, pl.ds(at, 3)]

        def make(dx, dz, px, pz):
            remote(mine, mine, plane_send.at[1, k], row_recv.at[k, dx], place(px, y, pz, core)).start()

        plane_copies(make)

    def line(k, d):
        return remote(r4.at[k, y], r4.at[k, y], line_send.at[k, d - 1], line_recv.at[k, d - 1], along_y[d - 1])

    def pair_sum(k):
        pair_out(k).wait_recv()
        s1[k] = acc[k, pl.ds(96 * core, 96)] + r1[k]
        plane_out(k)

    def plane_sum(k):
        whole(r2.at[k], plane_send.at[0, k], plane_recv.at[k]).wait_recv()
        total = s1[k, pl.ds(3 * (x * 8 + z), 3)]
        parts = [r2[k, d] for d in range(31)]
        while len(parts) > 1:
            parts = [a + b for a, b in zip(parts[::2], parts[1::2])] + ([parts[-1]] if len(parts) % 2 else [])
        r4[k, y] = total + parts[0]
        for d in (4, 3, 5, 2, 6, 1, 7):
            line(k, d).start()

    def line_sum(k):
        for d in range(1, 8):
            line(k, d).wait_recv()
        p = [r4[k, d] for d in range(8)]
        res[k, pl.ds(at, 3)] = ((p[0] + p[1]) + (p[2] + p[3])) + ((p[4] + p[5]) + (p[6] + p[7]))
        plane_back(k)

    def pair_back(k, dx):
        row = res.at[k, pl.ds(96 * core + 24 * lax.rem(x + 4 - dx, 4), 24)]
        return remote(row, row, pair_send.at[k, dx], pair_recv.at[k, dx], sibling)

    def gathered(k):
        for dx in (0, 1, 3, 2):
            rows = 21 if dx == 0 else 24
            whole(acc.at[k, pl.ds(0, rows)], plane_send.at[1, k], row_recv.at[k, dx]).wait_recv()
            pair_back(k, dx).start()

    def sent(k):
        pair_out(k).wait_send()
        whole(r2.at[k], plane_send.at[0, k], plane_recv.at[k]).wait_send()
        for d in range(1, 8):
            line(k, d).wait_send()

    def all_back(k):
        for dx in range(4):
            pair_back(k, dx).wait_recv()

    c = split(c_ref[0])
    fill(0, dot3(c, c, TN))
    pl.semaphore_wait(barrier, 39)
    pair_out(0).start()
    w = split(w_ref[:, 0, :])
    fill(1, dot3(w, w, NT))
    pair_out(1).start()
    pair_sum(0)
    turned = c_ref[0].T
    for q in range(6):
        t_refs[q][...] = turned[64*q:64*q+64, :]
    r_ref[...] = jnp.zeros_like(r_ref)
    pair_sum(1)
    plane_sum(0)
    plane_sum(1)
    line_sum(0)
    line_sum(1)
    gathered(0)
    sent(0)
    sent(1)
    all_back(0)

    def block(k, b):
        return res[k, 32*b:32*b+32].reshape(128, 128)

    for b, (i, j) in enumerate(PAIRS):
        a = block(0, b)
        a_refs[2*i][:, 128*j:128*j+128] = a[:64]
        a_refs[2*i+1][:, 128*j:128*j+128] = a[64:]
    for p in range(6):
        o = 128 * (p // 2)
        d = a_refs[p][:, o:o+128]
        if p % 2 == 0:
            d = pltpu.roll(d, 64, 1)
        (g,) = factor([single(d)], False)
        li = inverse(g)
        rp = dot6(li, a_refs[p][:, o:], NN)
        if p % 2:
            rp = jnp.where(lax.broadcasted_iota(jnp.int32, rp.shape, 1) >= 64, rp, 0.0)
        r_ref[64*p:64*p+64, o:] = rp
        ortho = dot3(li, t_refs[p][...], NN)
        ortho_ref[64*p:64*p+64, :] = ortho
        for q in range(p + 1, 6):
            oq = 128 * (q // 2)
            lq = rp[:, 64*q-o:64*q-o+64]
            a_refs[q][:, oq:] -= dot6(lq, rp[:, oq-o:], TN)
            t_refs[q][...] -= dot3(lq, ortho, TN)
        moved_ref[64*p:64*p+64, :] = dot3(rp, (w[0][o:, :], w[1][o:, :]), NN)
        if p == 1:
            gathered(1)
    all_back(1)
    for b, (i, j) in enumerate(PAIRS):
        a = block(1, b)
        m_ref[128*i:128*i+128, 128*j:128*j+128] = a
        if i < j:
            m_ref[128*j:128*j+128, 128*i:128*i+128] = a.T
    for k in range(2):
        whole(r2.at[k], plane_send.at[1, k], plane_recv.at[k]).wait_send()
        for dx in range(4):
            pair_back(k, dx).wait_send()


def first(core, nxt):
    v = pl.BlockSpec(memory_space=pltpu.VMEM)
    f32 = lambda *s: pltpu.VMEM(s, jnp.float32)
    half = lambda *lead: pltpu.VMEM(lead + (4, 128), jnp.float32)
    sems = pltpu.SemaphoreType.DMA
    square = jax.ShapeDtypeStruct((RANK, RANK), jnp.float32)
    return pl.pallas_call(
        sum_and_factor,
        out_shape=(square,) * 4,
        in_specs=[v] * 2, out_specs=(v,) * 4,
        scratch_shapes=[half(2, 192), half(2, 96), half(2, 96), half(2, 31, 3), half(2, 8, 3), half(2, 192)]
        + [f32(64, RANK)] * 12
        + [sems((2, 5)), sems((2, 5)), sems((2, 2)), sems((2,)), sems((2, 4)), sems((2, 7)), sems((2, 7))],
        compiler_params=pltpu.CompilerParams(collective_id=0, has_side_effects=True, vmem_limit_bytes=40 * 1024 * 1024),
    )(core, nxt)


def iterate(scale, r_ref, m_ref, ortho_ref, moved_ref, s_ref, co_ref, no_ref, bh_ref, bl_ref, y_ref, yh_ref, yl_ref, f_ref, *p_refs):
    r = r_ref[...]
    rs = split(r)
    a = jnp.concatenate([dot3(s_ref[...], rs, NN), r], axis=0)
    a = dot3(dot3(a, m_ref[...], NN), rs, NT)
    start = a[:192]
    bh_ref[...], bl_ref[...] = split(a[192:])
    y_ref[...] = jnp.zeros_like(y_ref)
    for j in range(4):
        y_ref[64*j:64*j+48, :] = start[48*j:48*j+48, :]
    yh_ref[...], yl_ref[...] = split(y_ref[...])
    for p in p_refs:
        p[...] = jnp.zeros_like(p)
    ph, pll = p_refs[:3], p_refs[3:]

    def wave(w, _):
        y = [y_ref[64*j:64*j+64, :] for j in range(4)]
        ys = [(yh_ref[64*j:64*j+64, :], yl_ref[64*j:64*j+64, :]) for j in range(4)]
        prev = [None] + [(ph[j][...], pll[j][...]) for j in range(3)]
        stack = lambda *parts: tuple(jnp.concatenate([q[i] for q in parts], axis=0) for i in range(2))
        left = lambda q: (q[0][:, :RANK], q[1][:, :RANK])
        e = [dot3(ys[0], stack(ys[0], ys[1]), NT), dot3(ys[1], stack(left(prev[1]), ys[1]), NT),
             dot3(ys[2], stack(left(prev[2]), ys[2], ys[3]), NT), dot3(ys[3], stack(left(prev[3]), ys[3]), NT)]
        c = [None] + [split(e[j][:, :64*j]) for j in range(1, 4)]
        s = [e[0]] + [e[j][:, -128:] - dot3(c[j], stack(c[j], c[j]), NT) for j in range(1, 4)]
        col = lax.broadcasted_iota(jnp.int32, (64, 128), 1)
        groups = factor([pair(jnp.where(col < 64, s[j], s[j+1])[:48]) for j in (0, 2)], False)
        image = dot3((yh_ref[...], yl_ref[...]), (bh_ref[...], bl_ref[...]), NN)
        x = [jnp.concatenate([y[j], image[64*j:64*j+64]], axis=1) for j in range(4)]
        x = [x[0]] + [x[j] - dot3(c[j], prev[j], NN) for j in range(1, 4)]
        n = [dot3(inverse(groups[i]), jnp.concatenate(x[2*i:2*i+2], axis=0), NN) for i in range(2)]
        n = [n[0][:64], n[0][64:], n[1][:64], n[1][64:]]
        for j in range(4):
            parts = split(n[j])
            if j < 3:
                for half, part in zip((ph, pll), parts):
                    for k in range(2, j, -1):
                        half[k][64*j:64*j+64, :] = half[k-1][64*j:64*j+64, :]
                    half[j][64*j:64*j+64, :] = part

            @pl.when(w - j < ITERS)
            def _(j=j):
                f_ref[48*j:48*j+48, :] = n[j][:48, :RANK]

            @pl.when(w >= j)
            def _(j=j, parts=parts):
                y_ref[64*j:64*j+64, :] = n[j][:, RANK:]
                yh_ref[64*j:64*j+64, :] = parts[0][:, RANK:]
                yl_ref[64*j:64*j+64, :] = parts[1][:, RANK:]
        return 0

    lax.fori_loop(0, ITERS + 3, wave, 0)
    f = split(f_ref[...])
    co_ref[...] = scale * dot3(f, ortho_ref[...], NN)
    no_ref[:, 0, :] = dot3(f, moved_ref[...], NN)


def second(r, m, ortho, moved, start, scale):
    v = pl.BlockSpec(memory_space=pltpu.VMEM)
    f32 = lambda *s: pltpu.VMEM(s, jnp.float32)
    bf16 = lambda *s: pltpu.VMEM(s, jnp.bfloat16)
    return pl.pallas_call(
        functools.partial(iterate, scale),
        out_shape=(jax.ShapeDtypeStruct((192, RANK), jnp.float32), jax.ShapeDtypeStruct((192, 1, RANK), jnp.float32)),
        in_specs=[v] * 5, out_specs=(v, v),
        scratch_shapes=[bf16(RANK, RANK), bf16(RANK, RANK), f32(256, RANK), bf16(256, RANK), bf16(256, RANK), f32(192, RANK)]
        + [bf16(64 * j, 2 * RANK) for j in (1, 2, 3, 1, 2, 3)],
        compiler_params=pltpu.CompilerParams(vmem_limit_bytes=40 * 1024 * 1024),
    )(r, m, ortho, moved, start)


def shards(core, next_core, start_block):
    r, m, ortho, moved = first(core, next_core)
    scale = math.sqrt(core.shape[0] * lax.axis_size("wide") * lax.axis_size("narrow") * core.shape[1])
    core_t, next_out = second(r, m, ortho, moved, start_block.T, scale)
    return core_t.T[None], next_out


def solution(mesh):
    placed = (P(("wide", "narrow"), None, None), P(None, ("wide", "narrow"), None), P())
    return jax.shard_map(
        shards,
        mesh=mesh,
        in_specs=placed,
        out_specs=(P(("wide", "narrow"), None, None), P(None, ("wide", "narrow"), None)),
        check_vma=False,
    )
```

```python
import functools
import math

import jax
import jax.numpy as jnp
from jax import lax
from jax.experimental import pallas as pl
from jax.experimental.pallas import tpu as pltpu
from jax.sharding import PartitionSpec as P

RANK = 384
ITERS = 6
MESH = pl.DeviceIdType.MESH
PAIRS = ((0, 0), (0, 1), (0, 2), (1, 1), (1, 2), (2, 2))
NN = (((1,), (0,)), ((), ()))
NT = (((1,), (1,)), ((), ()))
TN = (((0,), (0,)), ((), ()))


def split(a):
    hi = a.astype(jnp.bfloat16)
    return hi, (a - hi.astype(jnp.float32)).astype(jnp.bfloat16)


def dot3(a, b, dims):
    ah, al = a if isinstance(a, tuple) else split(a)
    bh, bl = b if isinstance(b, tuple) else split(b)
    one = lambda x, y: lax.dot_general(x, y, dims, preferred_element_type=jnp.float32)
    if dims == TN:
        return one(ah, bh) + (one(ah, bl) + one(al, bh))
    rows = ah.shape[0]
    both = one(jnp.concatenate([ah, al], axis=0), bh)
    return both[:rows] + (both[rows:] + one(ah, bl))


def row_of(v, j):
    return jnp.broadcast_to(v[j:j+1, :], (8, 128))


def factor(groups, gj):
    sub = lax.broadcasted_iota(jnp.int32, (8, 128), 0)
    lane_id = lax.broadcasted_iota(jnp.int32, (8, 128), 1)
    n = len(groups[0][1])

    def lanes(pair, X, t):
        if pair is not True:
            return [jnp.broadcast_to(X[:, pair+8*t+j:pair+8*t+j+1], (8, 128)) for j in range(8)]
        base = jnp.where(lane_id < 64, 0, 64)
        return [jnp.take_along_axis(X, base + (8*t + j), axis=1) for j in range(8)]

    ahead = [lanes(pair, tiles[0][0], 0) for pair, tiles in groups]
    for t in range(n):
        for g, (pair, A) in enumerate(groups):
            cb = ahead[g]
            P = A[t]
            W = list(P)
            dv = rv = None
            last = t + 1 == n
            if not last:
                X = A[t+1]
                cu = lanes(pair, X[0], t)
                cn = lanes(pair, X[0], t+1)
            others = range(t+2, n)
            if not gj:
                co = {u: lanes(pair, A[u][0], t) for u in others}
            for j in range(8):
                dj = row_of(cb[j], j)
                r = 1.0 / dj
                dv = dj if j == 0 else jnp.where(sub == j, dj, dv)
                rows = [row_of(p, j) for p in P]
                bs = {i: row_of(cb[j], i) for i in range(j+1, 8)}
                if gj:
                    rv = r if j == 0 else jnp.where(sub == j, r, rv)
                    mg = jnp.where(sub == j, 0.0, cb[j] * r)
                    W = [w - mg * x for w, x in zip(W, rows)]
                    mf = jnp.where(sub > j, mg, 0.0)
                else:
                    mg = mf = jnp.where(sub > j, cb[j] * r, 0.0)
                P = [p - mf * x for p, x in zip(P, rows)]
                for i in range(j+1, 8):
                    cb[i] = cb[i] - mg * bs[i]
                if not last:
                    m = cu[j] * r
                    X = [a - m * x for a, x in zip(X, rows)]
                    for i in range(8):
                        cn[i] = cn[i] - m * row_of(cu[j], i)
                    for i in range(j+1, 8):
                        cu[i] = cu[i] - m * bs[i]
                if not gj:
                    for u in others:
                        m = co[u][j] * r
                        A[u] = [a - m * x for a, x in zip(A[u], rows)]
                        for i in range(j+1, 8):
                            co[u][i] = co[u][i] - m * bs[i]
            s = lax.rsqrt(dv)
            A[t] = [p * s for p in P]
            if not last:
                A[t+1] = X
                ahead[g] = cn
            if gj and t + 2 < n:
                wr = [[row_of(w * rv, j) for j in range(8)] for w in W]
                for u in others:
                    co = lanes(pair, A[u][0], t)
                    new = []
                    for a, wv in zip(A[u], wr):
                        p = [co[j] * wv[j] for j in range(8)]
                        new.append(a - (((p[0] + p[1]) + (p[2] + p[3])) + ((p[4] + p[5]) + (p[6] + p[7]))))
                    A[u] = new
    return groups


def iotas(rows):
    return lax.broadcasted_iota(jnp.int32, (rows, 128), 0), lax.broadcasted_iota(jnp.int32, (rows, 128), 1)


def rows_of_tiles(*arrays):
    return [[a[8*t:8*t+8, :] for a in arrays] for t in range(8)]


def joined(tiles, i):
    return jnp.concatenate([t[i] for t in tiles], axis=0)


def pair(s):
    row, col = iotas(s.shape[0])
    eye = jnp.where((col == row) | (col == row + 64), 1.0, 0.0)
    return True, [[s[8*t:8*t+8, :], eye[8*t:8*t+8, :]] for t in range(s.shape[0] // 8)]


def inverse(group):
    a = joined(group[1], 1)
    if a.shape[0] < 64:
        a = jnp.concatenate([a, jnp.zeros((64 - a.shape[0], 128), jnp.float32)], axis=0)
    row, col = iotas(128)
    return jnp.where((row < 64) == (col < 64), jnp.concatenate([a, a], axis=0), 0.0)


def sum_and_factor(c_ref, next_hbm, r_ref, m_ref, v_ref, flat_ref, w_ref, acc, r1, s1, r2, r4, res, *more):
    a_refs = more[:6]
    in_sem, pair_send, pair_recv, plane_send, plane_recv, row_recv, line_send, line_recv = more[6:]
    wide, y = lax.axis_index("wide"), lax.axis_index("narrow")
    core, z, x = lax.rem(wide, 2), lax.rem(wide // 2, 8), wide // 16

    def place(x, y, z, core):
        return ((x * 8 + z) * 2 + core, y)

    def in_plane(d):
        return lax.rem(x + d // 8, 4), lax.rem(z + lax.rem(d, 8), 8)

    sibling = place(x, y, z, 1 - core)
    along_y = [place(x, lax.rem(y + d, 8), z, core) for d in range(1, 8)]

    load_w = pltpu.make_async_copy(next_hbm, w_ref, in_sem)
    load_w.start()
    barrier = pltpu.get_barrier_semaphore()
    for other in [sibling] + along_y:
        pl.semaphore_signal(barrier, inc=1, device_id=other, device_id_type=MESH)

    def greet(d, _):
        px, pz = in_plane(d)
        pl.semaphore_signal(barrier, inc=1, device_id=place(px, y, pz, core), device_id_type=MESH)
        return 0

    lax.fori_loop(1, 32, greet, 0)

    def remote(src, dst, send, recv, other):
        return pltpu.make_async_remote_copy(src_ref=src, dst_ref=dst, send_sem=send, recv_sem=recv, device_id=other, device_id_type=MESH)

    def fill(k, a):
        for b, (i, j) in enumerate(PAIRS):
            acc[k, 32*b:32*b+32] = a[128*i:128*i+128, 128*j:128*j+128].reshape(32, 4, 128)

    def whole(ref, send, recv):
        return remote(ref, ref, send, recv, sibling)

    def pair_out(k):
        return remote(acc.at[k, pl.ds(96 * (1 - core), 96)], r1.at[k], pair_send.at[k, 4], pair_recv.at[k, 4], sibling)

    at = 96 * core + 3 * (x * 8 + z)

    def plane_copies(make):
        for dx in (2, 1, 3, 0):
            def step(i, _, dx=dx):
                dz = 1 + lax.rem(2 + i, 7) if dx == 0 else lax.rem(4 + i, 8)
                make(dx, dz, lax.rem(x + dx, 4), lax.rem(z + dz, 8))
                return 0

            lax.fori_loop(1 if dx == 0 else 0, 8, step, 0, unroll=True)

    def plane_out(k):
        def make(dx, dz, px, pz):
            remote(s1.at[k, pl.ds(3 * (px * 8 + pz), 3)], r2.at[k, dx * 8 + dz - 1], plane_send.at[0, k], plane_recv.at[k],
                   place(px, y, pz, core)).start()

        plane_copies(make)

    def plane_back(k):
        mine = res.at[k, pl.ds(at, 3)]

        def make(dx, dz, px, pz):
            remote(mine, mine, plane_send.at[1, k], row_recv.at[k, dx], place(px, y, pz, core)).start()

        plane_copies(make)

    def line(k, d):
        return remote(r4.at[k, y], r4.at[k, y], line_send.at[k, d - 1], line_recv.at[k, d - 1], along_y[d - 1])

    def pair_sum(k):
        pair_out(k).wait_recv()
        s1[k] = acc[k, pl.ds(96 * core, 96)] + r1[k]
        plane_out(k)

    def plane_sum(k):
        whole(r2.at[k], plane_send.at[0, k], plane_recv.at[k]).wait_recv()
        total = s1[k, pl.ds(3 * (x * 8 + z), 3)]
        parts = [r2[k, d] for d in range(31)]
        while len(parts) > 1:
            parts = [a + b for a, b in zip(parts[::2], parts[1::2])] + ([parts[-1]] if len(parts) % 2 else [])
        r4[k, y] = total + parts[0]
        for d in (4, 3, 5, 2, 6, 1, 7):
            line(k, d).start()

    def line_sum(k):
        for d in range(1, 8):
            line(k, d).wait_recv()
        p = [r4[k, d] for d in range(8)]
        res[k, pl.ds(at, 3)] = ((p[0] + p[1]) + (p[2] + p[3])) + ((p[4] + p[5]) + (p[6] + p[7]))
        plane_back(k)

    def pair_back(k, dx):
        row = res.at[k, pl.ds(96 * core + 24 * lax.rem(x + 4 - dx, 4), 24)]
        return remote(row, row, pair_send.at[k, dx], pair_recv.at[k, dx], sibling)

    def gathered(k):
        for dx in (0, 1, 3, 2):
            rows = 21 if dx == 0 else 24
            whole(acc.at[k, pl.ds(0, rows)], plane_send.at[1, k], row_recv.at[k, dx]).wait_recv()
            pair_back(k, dx).start()

    def sent(k):
        pair_out(k).wait_send()
        whole(r2.at[k], plane_send.at[0, k], plane_recv.at[k]).wait_send()
        for d in range(1, 8):
            line(k, d).wait_send()

    def all_back(k):
        for dx in range(4):
            pair_back(k, dx).wait_recv()

    c = split(c_ref[0])
    fill(0, dot3(c, c, TN))
    pl.semaphore_wait(barrier, 39)
    pair_out(0).start()
    pair_sum(0)
    load_w.wait()
    w = w_ref[:, 0, :]
    flat_ref[...] = w
    w = split(w)
    fill(1, dot3(w, w, NT))
    pair_out(1).start()
    v_ref[...] = jnp.zeros_like(v_ref)
    r_ref[...] = jnp.zeros_like(r_ref)
    pair_sum(1)
    plane_sum(0)
    plane_sum(1)
    line_sum(0)
    line_sum(1)
    gathered(0)
    sent(0)
    sent(1)
    all_back(0)

    def block(k, b):
        return res[k, 32*b:32*b+32].reshape(128, 128)

    for b, (i, j) in enumerate(PAIRS):
        a = block(0, b)
        a_refs[2*i][:, 128*j:128*j+128] = a[:64]
        a_refs[2*i+1][:, 128*j:128*j+128] = a[64:]
    row, col = iotas(64)
    eye = jnp.where(col == row, 1.0, 0.0)
    for p in range(6):
        o = 128 * (p // 2)
        here = a_refs[p][:, o:o+128]
        if p % 2 == 0:
            ((_, tiles),) = factor([(0, rows_of_tiles(here, eye))], False)
            own = joined(tiles, 1)
            li = own[:, :64]
            near = joined(tiles, 0)
            near = jnp.where((col >= 64) | (col >= row), near, 0.0)
            r_ref[64*p:64*p+64, o:o+128] = near
            rp = near
            a_refs[p+1][:, o:o+128] -= dot3(near[:, 64:], near, TN)
            far = o + 128
        else:
            more_tiles = [a_refs[p][:, o+128:o+256]] if p < 5 else []
            ((_, tiles),) = factor([(64, rows_of_tiles(jnp.where(col >= 64, here, eye), *more_tiles))], False)
            first_tile = joined(tiles, 0)
            li = first_tile[:, :64]
            own = pltpu.roll(jnp.where(col < 64, first_tile, 0.0), 64, 1)
            r_ref[64*p:64*p+64, o:o+128] = jnp.where(col - 64 >= row, first_tile, 0.0)
            rp = jnp.where(col - 64 >= row, first_tile, 0.0)
            if p < 5:
                near = joined(tiles, 1)
                r_ref[64*p:64*p+64, o+128:o+256] = near
                rp = jnp.concatenate([rp, near], axis=1)
                a_refs[p+1][:, o+128:o+256] -= dot3(near[:, :64], near, TN)
            far = o + 256
        if far < RANK:
            rest = dot3(li, a_refs[p][:, far:], NN)
            r_ref[64*p:64*p+64, far:] = rest
            rp = jnp.concatenate([rp, rest], axis=1)
        for q in range(p + 1, 6):
            oq = 128 * (q // 2)
            lq = rp[:, 64*q-o:64*q-o+64]
            if q == p + 1:
                oq += 128
            if oq < RANK:
                a_refs[q][:, oq:] -= dot3(lq, rp[:, oq-o:], TN)
        if p:
            earlier = dot3(r_ref[:64*p, 64*p:64*p+64], v_ref[:64*p, :o+128], TN)
            v_ref[64*p:64*p+64, :o+128] = -dot3(li, earlier, NN)
        v_ref[64*p:64*p+64, o:o+128] += own
        if p == 1:
            gathered(1)
    all_back(1)
    for b, (i, j) in enumerate(PAIRS):
        a = block(1, b)
        m_ref[128*i:128*i+128, 128*j:128*j+128] = a
        if i < j:
            m_ref[128*j:128*j+128, 128*i:128*i+128] = a.T
    for k in range(2):
        whole(r2.at[k], plane_send.at[1, k], plane_recv.at[k]).wait_send()
        for dx in range(4):
            pair_back(k, dx).wait_send()


def first(core, nxt):
    v = pl.BlockSpec(memory_space=pltpu.VMEM)
    f32 = lambda *s: pltpu.VMEM(s, jnp.float32)
    half = lambda *lead: pltpu.VMEM(lead + (4, 128), jnp.float32)
    sems = pltpu.SemaphoreType.DMA
    square = jax.ShapeDtypeStruct((RANK, RANK), jnp.float32)
    return pl.pallas_call(
        sum_and_factor,
        out_shape=(square,) * 4,
        in_specs=[v, pl.BlockSpec(memory_space=pl.ANY)], out_specs=(v,) * 4,
        scratch_shapes=[f32(RANK, 1, RANK), half(2, 192), half(2, 96), half(2, 96), half(2, 31, 3), half(2, 8, 3), half(2, 192)]
        + [f32(64, RANK)] * 6
        + [sems(()), sems((2, 5)), sems((2, 5)), sems((2, 2)), sems((2,)), sems((2, 4)), sems((2, 7)), sems((2, 7))],
        compiler_params=pltpu.CompilerParams(collective_id=0, has_side_effects=True, vmem_limit_bytes=51 * 1024 * 1024),
    )(core, nxt)


def iterate(scale, r_ref, m_ref, v_ref, w_ref, s_ref, c_ref, co_ref, no_ref, bh_ref, bl_ref, y_ref, yh_ref, yl_ref, f_ref, *p_refs):
    r = r_ref[...]
    rs = split(r)
    a = jnp.concatenate([dot3(s_ref[...], rs, NN), r], axis=0)
    a = dot3(dot3(a, m_ref[...], NN), rs, NT)
    start = a[:192]
    bh_ref[...], bl_ref[...] = split(a[192:])
    y_ref[...] = jnp.zeros_like(y_ref)
    for j in range(4):
        y_ref[64*j:64*j+48, :] = start[48*j:48*j+48, :]
    yh_ref[...], yl_ref[...] = split(y_ref[...])
    for p in p_refs:
        p[...] = jnp.zeros_like(p)
    ph, pll = p_refs[:3], p_refs[3:]

    def wave(w, _):
        y = [y_ref[64*j:64*j+64, :] for j in range(4)]
        ys = [(yh_ref[64*j:64*j+64, :], yl_ref[64*j:64*j+64, :]) for j in range(4)]
        prev = [None] + [(ph[j][...], pll[j][...]) for j in range(3)]
        stack = lambda *parts: tuple(jnp.concatenate([q[i] for q in parts], axis=0) for i in range(2))
        left = lambda q: (q[0][:, :RANK], q[1][:, :RANK])
        e = [dot3(ys[0], stack(ys[0], ys[1]), NT), dot3(ys[1], stack(left(prev[1]), ys[1]), NT),
             dot3(ys[2], stack(left(prev[2]), ys[2], ys[3]), NT), dot3(ys[3], stack(left(prev[3]), ys[3]), NT)]
        c = [None] + [split(e[j][:, :64*j]) for j in range(1, 4)]
        s = [e[0]] + [e[j][:, -128:] - dot3(c[j], stack(c[j], c[j]), NT) for j in range(1, 4)]
        col = lax.broadcasted_iota(jnp.int32, (64, 128), 1)
        groups = factor([pair(jnp.where(col < 64, s[j], s[j+1])[:48]) for j in (0, 2)], False)
        image = dot3((yh_ref[...], yl_ref[...]), (bh_ref[...], bl_ref[...]), NN)
        x = [jnp.concatenate([y[j], image[64*j:64*j+64]], axis=1) for j in range(4)]
        x = [x[0]] + [x[j] - dot3(c[j], prev[j], NN) for j in range(1, 4)]
        n = [dot3(inverse(groups[i]), jnp.concatenate(x[2*i:2*i+2], axis=0), NN) for i in range(2)]
        n = [n[0][:64], n[0][64:], n[1][:64], n[1][64:]]
        for j in range(4):
            parts = split(n[j])
            if j < 3:
                for half, part in zip((ph, pll), parts):
                    for k in range(2, j, -1):
                        half[k][64*j:64*j+64, :] = half[k-1][64*j:64*j+64, :]
                    half[j][64*j:64*j+64, :] = part

            @pl.when(w - j < ITERS)
            def _(j=j):
                f_ref[48*j:48*j+48, :] = n[j][:48, :RANK]

            @pl.when(w >= j)
            def _(j=j, parts=parts):
                y_ref[64*j:64*j+64, :] = n[j][:, RANK:]
                yh_ref[64*j:64*j+64, :] = parts[0][:, RANK:]
                yl_ref[64*j:64*j+64, :] = parts[1][:, RANK:]
        return 0

    lax.fori_loop(0, ITERS + 3, wave, 0)
    f = split(f_ref[...])
    co_ref[...] = scale * dot3(dot3(f, v_ref[...], NN), c_ref[0], NT)
    no_ref[:, 0, :] = dot3(dot3(f, r_ref[...], NN), w_ref[...], NN)


def second(r, m, v, w, start, core, scale):
    vmem = pl.BlockSpec(memory_space=pltpu.VMEM)
    f32 = lambda *s: pltpu.VMEM(s, jnp.float32)
    bf16 = lambda *s: pltpu.VMEM(s, jnp.bfloat16)
    return pl.pallas_call(
        functools.partial(iterate, scale),
        out_shape=(jax.ShapeDtypeStruct((192, RANK), jnp.float32), jax.ShapeDtypeStruct((192, 1, RANK), jnp.float32)),
        in_specs=[vmem] * 6, out_specs=(vmem, vmem),
        scratch_shapes=[bf16(RANK, RANK), bf16(RANK, RANK), f32(256, RANK), bf16(256, RANK), bf16(256, RANK), f32(192, RANK)]
        + [bf16(64 * j, 2 * RANK) for j in (1, 2, 3, 1, 2, 3)],
        compiler_params=pltpu.CompilerParams(vmem_limit_bytes=40 * 1024 * 1024),
    )(r, m, v, w, start, core)


def shards(core, next_core, start_block):
    r, m, v, w = first(core, next_core)
    scale = math.sqrt(core.shape[0] * lax.axis_size("wide") * lax.axis_size("narrow") * core.shape[1])
    core_t, next_out = second(r, m, v, w, start_block.T, core, scale)
    return core_t.T[None], next_out


def solution(mesh):
    placed = (P(("wide", "narrow"), None, None), P(None, ("wide", "narrow"), None), P())
    return jax.shard_map(
        shards,
        mesh=mesh,
        in_specs=placed,
        out_specs=(P(("wide", "narrow"), None, None), P(None, ("wide", "narrow"), None)),
        check_vma=False,
    )
```

```python
import functools
import math

import jax
import jax.numpy as jnp
from jax import lax
from jax.experimental import pallas as pl
from jax.experimental.pallas import tpu as pltpu
from jax.sharding import PartitionSpec as P

RANK = 384
ITERS = 6
MESH = pl.DeviceIdType.MESH
PAIRS = ((0, 0), (0, 1), (0, 2), (1, 1), (1, 2), (2, 2))
NN = (((1,), (0,)), ((), ()))
NT = (((1,), (1,)), ((), ()))
TN = (((0,), (0,)), ((), ()))


def split(a):
    hi = a.astype(jnp.bfloat16)
    return hi, (a - hi.astype(jnp.float32)).astype(jnp.bfloat16)


def dot3(a, b, dims):
    ah, al = a if isinstance(a, tuple) else split(a)
    bh, bl = b if isinstance(b, tuple) else split(b)
    one = lambda x, y: lax.dot_general(x, y, dims, preferred_element_type=jnp.float32)
    if dims == TN:
        return one(ah, bh) + (one(ah, bl) + one(al, bh))
    rows = ah.shape[0]
    both = one(jnp.concatenate([ah, al], axis=0), bh)
    return both[:rows] + (both[rows:] + one(ah, bl))


def row_of(v, j):
    return jnp.broadcast_to(v[j:j+1, :], (8, 128))


def factor(groups, gj):
    sub = lax.broadcasted_iota(jnp.int32, (8, 128), 0)
    lane_id = lax.broadcasted_iota(jnp.int32, (8, 128), 1)
    n = len(groups[0][1])

    def lanes(pair, X, t):
        if pair is not True:
            return [jnp.broadcast_to(X[:, pair+8*t+j:pair+8*t+j+1], (8, 128)) for j in range(8)]
        base = jnp.where(lane_id < 64, 0, 64)
        return [jnp.take_along_axis(X, base + (8*t + j), axis=1) for j in range(8)]

    ahead = [lanes(pair, tiles[0][0], 0) for pair, tiles in groups]
    for t in range(n):
        for g, (pair, A) in enumerate(groups):
            cb = ahead[g]
            P = A[t]
            W = list(P)
            dv = rv = None
            last = t + 1 == n
            if not last:
                X = A[t+1]
                cu = lanes(pair, X[0], t)
                cn = lanes(pair, X[0], t+1)
            others = range(t+2, n)
            if not gj:
                co = {u: lanes(pair, A[u][0], t) for u in others}
            dj = row_of(cb[0], 0)
            for j in range(8):
                r = 1.0 / dj
                dv = dj if j == 0 else jnp.where(sub == j, dj, dv)
                rows = [row_of(p, j) for p in P]
                bs = {i: row_of(cb[j], i) for i in range(j+1, 8)}
                if j < 7:
                    dj = row_of(cb[j+1], j+1) - (bs[j+1] * bs[j+1]) * r
                if gj:
                    rv = r if j == 0 else jnp.where(sub == j, r, rv)
                    mg = jnp.where(sub == j, 0.0, cb[j] * r)
                    W = [w - mg * x for w, x in zip(W, rows)]
                    mf = jnp.where(sub > j, mg, 0.0)
                else:
                    mg = mf = jnp.where(sub > j, cb[j] * r, 0.0)
                P = [p - mf * x for p, x in zip(P, rows)]
                for i in range(j+1, 8):
                    cb[i] = cb[i] - mg * bs[i]
                if not last:
                    m = cu[j] * r
                    X = [a - m * x for a, x in zip(X, rows)]
                    for i in range(8):
                        cn[i] = cn[i] - m * row_of(cu[j], i)
                    for i in range(j+1, 8):
                        cu[i] = cu[i] - m * bs[i]
                if not gj:
                    for u in others:
                        m = co[u][j] * r
                        A[u] = [a - m * x for a, x in zip(A[u], rows)]
                        for i in range(j+1, 8):
                            co[u][i] = co[u][i] - m * bs[i]
            s = lax.rsqrt(dv)
            A[t] = [p * s for p in P]
            if not last:
                A[t+1] = X
                ahead[g] = cn
            if gj and t + 2 < n:
                wr = [[row_of(w * rv, j) for j in range(8)] for w in W]
                for u in others:
                    co = lanes(pair, A[u][0], t)
                    new = []
                    for a, wv in zip(A[u], wr):
                        p = [co[j] * wv[j] for j in range(8)]
                        new.append(a - (((p[0] + p[1]) + (p[2] + p[3])) + ((p[4] + p[5]) + (p[6] + p[7]))))
                    A[u] = new
    return groups


def iotas(rows):
    return lax.broadcasted_iota(jnp.int32, (rows, 128), 0), lax.broadcasted_iota(jnp.int32, (rows, 128), 1)


def rows_of_tiles(*arrays):
    return [[a[8*t:8*t+8, :] for a in arrays] for t in range(8)]


def joined(tiles, i):
    return jnp.concatenate([t[i] for t in tiles], axis=0)


def pair(s):
    row, col = iotas(s.shape[0])
    eye = jnp.where((col == row) | (col == row + 64), 1.0, 0.0)
    return True, [[s[8*t:8*t+8, :], eye[8*t:8*t+8, :]] for t in range(s.shape[0] // 8)]


def inverse(group):
    a = joined(group[1], 1)
    if a.shape[0] < 64:
        a = jnp.concatenate([a, jnp.zeros((64 - a.shape[0], 128), jnp.float32)], axis=0)
    row, col = iotas(128)
    return jnp.where((row < 64) == (col < 64), jnp.concatenate([a, a], axis=0), 0.0)


def sum_and_factor(c_ref, next_hbm, r_ref, rm_ref, v_ref, flat_ref, w_ref, m_ref, acc, r1, s1, r2, r4, res, *more):
    a_refs = more[:6]
    in_sem, pair_send, pair_recv, plane_send, plane_recv, row_recv, line_send, line_recv = more[6:]
    wide, y = lax.axis_index("wide"), lax.axis_index("narrow")
    core, z, x = lax.rem(wide, 2), lax.rem(wide // 2, 8), wide // 16

    def place(x, y, z, core):
        return ((x * 8 + z) * 2 + core, y)

    def in_plane(d):
        return lax.rem(x + d // 8, 4), lax.rem(z + lax.rem(d, 8), 8)

    sibling = place(x, y, z, 1 - core)
    along_y = [place(x, lax.rem(y + d, 8), z, core) for d in range(1, 8)]

    load_w = pltpu.make_async_copy(next_hbm, w_ref, in_sem)
    load_w.start()
    barrier = pltpu.get_barrier_semaphore()
    for other in [sibling] + along_y:
        pl.semaphore_signal(barrier, inc=1, device_id=other, device_id_type=MESH)

    def greet(d, _):
        px, pz = in_plane(d)
        pl.semaphore_signal(barrier, inc=1, device_id=place(px, y, pz, core), device_id_type=MESH)
        return 0

    lax.fori_loop(1, 32, greet, 0)

    def remote(src, dst, send, recv, other):
        return pltpu.make_async_remote_copy(src_ref=src, dst_ref=dst, send_sem=send, recv_sem=recv, device_id=other, device_id_type=MESH)

    def fill(k, a):
        for b, (i, j) in enumerate(PAIRS):
            acc[k, 32*b:32*b+32] = a[128*i:128*i+128, 128*j:128*j+128].reshape(32, 4, 128)

    def whole(ref, send, recv):
        return remote(ref, ref, send, recv, sibling)

    def pair_out(k):
        return remote(acc.at[k, pl.ds(96 * (1 - core), 96)], r1.at[k], pair_send.at[k, 4], pair_recv.at[k, 4], sibling)

    at = 96 * core + 3 * (x * 8 + z)

    def plane_copies(make):
        for dx in (2, 1, 3, 0):
            def step(i, _, dx=dx):
                dz = 1 + lax.rem(2 + i, 7) if dx == 0 else lax.rem(4 + i, 8)
                make(dx, dz, lax.rem(x + dx, 4), lax.rem(z + dz, 8))
                return 0

            lax.fori_loop(1 if dx == 0 else 0, 8, step, 0, unroll=True)

    def plane_out(k):
        def make(dx, dz, px, pz):
            remote(s1.at[k, pl.ds(3 * (px * 8 + pz), 3)], r2.at[k, dx * 8 + dz - 1], plane_send.at[0, k], plane_recv.at[k],
                   place(px, y, pz, core)).start()

        plane_copies(make)

    def plane_back(k):
        mine = res.at[k, pl.ds(at, 3)]

        def make(dx, dz, px, pz):
            remote(mine, mine, plane_send.at[1, k], row_recv.at[k, dx], place(px, y, pz, core)).start()

        plane_copies(make)

    def line(k, d):
        return remote(r4.at[k, y], r4.at[k, y], line_send.at[k, d - 1], line_recv.at[k, d - 1], along_y[d - 1])

    def pair_sum(k):
        pair_out(k).wait_recv()
        s1[k] = acc[k, pl.ds(96 * core, 96)] + r1[k]
        plane_out(k)

    def plane_sum(k):
        whole(r2.at[k], plane_send.at[0, k], plane_recv.at[k]).wait_recv()
        total = s1[k, pl.ds(3 * (x * 8 + z), 3)]
        parts = [r2[k, d] for d in range(31)]
        while len(parts) > 1:
            parts = [a + b for a, b in zip(parts[::2], parts[1::2])] + ([parts[-1]] if len(parts) % 2 else [])
        r4[k, y] = total + parts[0]
        for d in (4, 3, 5, 2, 6, 1, 7):
            line(k, d).start()

    def line_sum(k):
        for d in range(1, 8):
            line(k, d).wait_recv()
        p = [r4[k, d] for d in range(8)]
        res[k, pl.ds(at, 3)] = ((p[0] + p[1]) + (p[2] + p[3])) + ((p[4] + p[5]) + (p[6] + p[7]))
        plane_back(k)

    def pair_back(k, dx):
        row = res.at[k, pl.ds(96 * core + 24 * lax.rem(x + 4 - dx, 4), 24)]
        return remote(row, row, pair_send.at[k, dx], pair_recv.at[k, dx], sibling)

    def gathered(k):
        for dx in (0, 1, 3, 2):
            rows = 21 if dx == 0 else 24
            whole(acc.at[k, pl.ds(0, rows)], plane_send.at[1, k], row_recv.at[k, dx]).wait_recv()
            pair_back(k, dx).start()

    def sent(k):
        pair_out(k).wait_send()
        whole(r2.at[k], plane_send.at[0, k], plane_recv.at[k]).wait_send()
        for d in range(1, 8):
            line(k, d).wait_send()

    def all_back(k):
        for dx in range(4):
            pair_back(k, dx).wait_recv()

    c = split(c_ref[0])
    fill(0, dot3(c, c, TN))
    pl.semaphore_wait(barrier, 39)
    pair_out(0).start()
    pair_sum(0)
    load_w.wait()
    w = w_ref[:, 0, :]
    flat_ref[...] = w
    w = split(w)
    fill(1, dot3(w, w, NT))
    pair_out(1).start()
    v_ref[...] = jnp.zeros_like(v_ref)
    r_ref[...] = jnp.zeros_like(r_ref)
    pair_sum(1)
    plane_sum(0)
    plane_sum(1)
    line_sum(0)
    line_sum(1)
    gathered(0)
    sent(0)
    sent(1)
    all_back(0)

    def block(k, b):
        return res[k, 32*b:32*b+32].reshape(128, 128)

    for b, (i, j) in enumerate(PAIRS):
        a = block(0, b)
        a_refs[2*i][:, 128*j:128*j+128] = a[:64]
        a_refs[2*i+1][:, 128*j:128*j+128] = a[64:]
    row, col = iotas(64)
    eye = jnp.where(col == row, 1.0, 0.0)
    for p in range(6):
        o = 128 * (p // 2)
        here = a_refs[p][:, o:o+128]
        if p % 2 == 0:
            ((_, tiles),) = factor([(0, rows_of_tiles(here, eye))], False)
            own = joined(tiles, 1)
            li = own[:, :64]
            near = joined(tiles, 0)
            near = jnp.where((col >= 64) | (col >= row), near, 0.0)
            r_ref[64*p:64*p+64, o:o+128] = near
            rp = near
            a_refs[p+1][:, o:o+128] -= dot3(near[:, 64:], near, TN)
            far = o + 128
        else:
            more_tiles = [a_refs[p][:, o+128:o+256]] if p < 5 else []
            ((_, tiles),) = factor([(64, rows_of_tiles(jnp.where(col >= 64, here, eye), *more_tiles))], False)
            first_tile = joined(tiles, 0)
            li = first_tile[:, :64]
            own = pltpu.roll(jnp.where(col < 64, first_tile, 0.0), 64, 1)
            r_ref[64*p:64*p+64, o:o+128] = jnp.where(col - 64 >= row, first_tile, 0.0)
            rp = jnp.where(col - 64 >= row, first_tile, 0.0)
            if p < 5:
                near = joined(tiles, 1)
                r_ref[64*p:64*p+64, o+128:o+256] = near
                rp = jnp.concatenate([rp, near], axis=1)
                a_refs[p+1][:, o+128:o+256] -= dot3(near[:, :64], near, TN)
            far = o + 256
        if far < RANK:
            rest = dot3(li, a_refs[p][:, far:], NN)
            r_ref[64*p:64*p+64, far:] = rest
            rp = jnp.concatenate([rp, rest], axis=1)
        for q in range(p + 1, 6):
            oq = 128 * (q // 2)
            lq = rp[:, 64*q-o:64*q-o+64]
            if q == p + 1:
                oq += 128
            if oq < RANK:
                a_refs[q][:, oq:] -= dot3(lq, rp[:, oq-o:], TN)
        if p:
            earlier = dot3(r_ref[:64*p, 64*p:64*p+64], v_ref[:64*p, :o+128], TN)
            v_ref[64*p:64*p+64, :o+128] = -dot3(li, earlier, NN)
        v_ref[64*p:64*p+64, o:o+128] += own
        if p == 1:
            gathered(1)
        if p == 3:
            all_back(1)
            for b, (i, j) in enumerate(PAIRS):
                a = block(1, b)
                m_ref[128*i:128*i+128, 128*j:128*j+128] = a
                if i < j:
                    m_ref[128*j:128*j+128, 128*i:128*i+128] = a.T
            rm_ref[:256, :] = dot3(r_ref[:256, :], m_ref[...], NN)
        if p > 3:
            rm_ref[64*p:64*p+64, :] = dot3(rp, m_ref[o:, :], NN)
    for k in range(2):
        whole(r2.at[k], plane_send.at[1, k], plane_recv.at[k]).wait_send()
        for dx in range(4):
            pair_back(k, dx).wait_send()


def first(core, nxt):
    v = pl.BlockSpec(memory_space=pltpu.VMEM)
    f32 = lambda *s: pltpu.VMEM(s, jnp.float32)
    half = lambda *lead: pltpu.VMEM(lead + (4, 128), jnp.float32)
    sems = pltpu.SemaphoreType.DMA
    square = jax.ShapeDtypeStruct((RANK, RANK), jnp.float32)
    return pl.pallas_call(
        sum_and_factor,
        out_shape=(square,) * 4,
        in_specs=[v, pl.BlockSpec(memory_space=pl.ANY)], out_specs=(v,) * 4,
        scratch_shapes=[f32(RANK, 1, RANK), f32(RANK, RANK), half(2, 192), half(2, 96), half(2, 96), half(2, 31, 3), half(2, 8, 3), half(2, 192)]
        + [f32(64, RANK)] * 6
        + [sems(()), sems((2, 5)), sems((2, 5)), sems((2, 2)), sems((2,)), sems((2, 4)), sems((2, 7)), sems((2, 7))],
        compiler_params=pltpu.CompilerParams(collective_id=0, has_side_effects=True, vmem_limit_bytes=51 * 1024 * 1024),
    )(core, nxt)


def iterate(scale, r_ref, rm_ref, v_ref, w_ref, s_ref, c_ref, co_ref, no_ref):
    rm = rm_ref[...]
    a = dot3(jnp.concatenate([dot3(s_ref[...], rm, NN), rm], axis=0), r_ref[...], NT)
    bond = split(a[192:])
    pad = jnp.zeros((16, RANK), jnp.float32)
    stack = lambda *parts: tuple(jnp.concatenate([q[i] for q in parts], axis=0) for i in range(2))
    left = lambda q: (q[0][:, :RANK], q[1][:, :RANK])
    row, col = iotas(64)
    eyes = jnp.where((col == row) | (col == row + 64), 1.0, 0.0)
    y = [jnp.concatenate([a[48*j:48*j+48], pad], axis=0) for j in range(4)]
    ys = [split(v) for v in y]
    done, basis = {}, [None] * 4
    for w in range(ITERS + 3):
        turn = {j: w - j for j in range(4) if 0 <= w - j < ITERS}
        prev, c, s = {}, {}, {}
        for j, k in turn.items():
            if j == 0:
                s[j] = dot3(ys[j], stack(ys[j], ys[j]), NT)
                continue
            prev[j] = stack(*[done[i, k] for i in range(j)])
            e = dot3(ys[j], stack(left(prev[j]), ys[j], *([ys[j]] if j == 2 else [])), NT)
            c[j] = split(e[:, :64*j])
            s[j] = e[:, -128:] - dot3(c[j], stack(c[j], c[j]), NT)
        pairs = [i for i in (0, 2) if i in turn or i + 1 in turn]
        groups = factor([pair(jnp.where(col < 64, s.get(i, eyes), s.get(i + 1, eyes))[:48]) for i in pairs], False)
        onward = [j for j, k in turn.items() if k < ITERS - 1]
        image = dot3(stack(*[ys[j] for j in onward]), bond, NN) if onward else None
        for i, group in zip(pairs, groups):
            wide = any(j in onward for j in (i, i + 1))
            xs = []
            for j in (i, i + 1):
                if j in onward:
                    at = 64 * onward.index(j)
                    x = jnp.concatenate([y[j], image[at:at+64]], axis=1)
                elif j in turn:
                    x = y[j]
                else:
                    x = jnp.zeros((64, 2 * RANK if wide else RANK), jnp.float32)
                if j in prev:
                    x = x - dot3(c[j], prev[j] if j in onward else left(prev[j]), NN)
                if wide and x.shape[1] == RANK:
                    x = jnp.concatenate([x, jnp.zeros((64, RANK), jnp.float32)], axis=1)
                xs.append(x)
            n = dot3(inverse(group), jnp.concatenate(xs, axis=0), NN)
            for j in (i, i + 1):
                if j not in turn:
                    continue
                own = n[64*(j-i):64*(j-i)+64]
                done[j, turn[j]] = split(own if j in onward else own[:, :RANK])
                if j in onward:
                    y[j] = own[:, RANK:]
                    ys[j] = tuple(q[:, RANK:] for q in done[j, turn[j]])
                else:
                    basis[j] = own[:48, :RANK]
    f = split(jnp.concatenate(basis, axis=0))
    co_ref[...] = scale * dot3(dot3(f, v_ref[...], NN), c_ref[0], NT)
    no_ref[:, 0, :] = dot3(dot3(f, r_ref[...], NN), w_ref[...], NN)


def second(r, rm, v, w, start, core, scale):
    vmem = pl.BlockSpec(memory_space=pltpu.VMEM)
    return pl.pallas_call(
        functools.partial(iterate, scale),
        out_shape=(jax.ShapeDtypeStruct((192, RANK), jnp.float32), jax.ShapeDtypeStruct((192, 1, RANK), jnp.float32)),
        in_specs=[vmem] * 6, out_specs=(vmem, vmem),
        compiler_params=pltpu.CompilerParams(vmem_limit_bytes=40 * 1024 * 1024),
    )(r, rm, v, w, start, core)


def shards(core, next_core, start_block):
    r, rm, v, w = first(core, next_core)
    scale = math.sqrt(core.shape[0] * lax.axis_size("wide") * lax.axis_size("narrow") * core.shape[1])
    core_t, next_out = second(r, rm, v, w, start_block.T, core, scale)
    return core_t.T[None], next_out


def solution(mesh):
    placed = (P(("wide", "narrow"), None, None), P(None, ("wide", "narrow"), None), P())
    return jax.shard_map(
        shards,
        mesh=mesh,
        in_specs=placed,
        out_specs=(P(("wide", "narrow"), None, None), P(None, ("wide", "narrow"), None)),
        check_vma=False,
    )
```

```python
import functools
import math

import jax
import jax.numpy as jnp
from jax import lax
from jax.experimental import pallas as pl
from jax.experimental.pallas import tpu as pltpu
from jax.sharding import PartitionSpec as P

RANK = 384
ITERS = 6
MESH = pl.DeviceIdType.MESH
PAIRS = ((0, 0), (0, 1), (0, 2), (1, 1), (1, 2), (2, 2))
NN = (((1,), (0,)), ((), ()))
NT = (((1,), (1,)), ((), ()))
TN = (((0,), (0,)), ((), ()))


def split(a):
    hi = a.astype(jnp.bfloat16)
    return hi, (a - hi.astype(jnp.float32)).astype(jnp.bfloat16)


def dot3(a, b, dims):
    ah, al = a if isinstance(a, tuple) else split(a)
    bh, bl = b if isinstance(b, tuple) else split(b)
    one = lambda x, y: lax.dot_general(x, y, dims, preferred_element_type=jnp.float32)
    if dims == TN:
        return one(ah, bh) + (one(ah, bl) + one(al, bh))
    rows = ah.shape[0]
    both = one(jnp.concatenate([ah, al], axis=0), bh)
    return both[:rows] + (both[rows:] + one(ah, bl))


def row_of(v, j):
    return jnp.broadcast_to(v[j:j+1, :], (8, 128))


def factor(groups, gj):
    sub = lax.broadcasted_iota(jnp.int32, (8, 128), 0)
    lane_id = lax.broadcasted_iota(jnp.int32, (8, 128), 1)
    n = len(groups[0][1])

    def lanes(pair, X, t):
        if pair is not True:
            return [jnp.broadcast_to(X[:, pair+8*t+j:pair+8*t+j+1], (8, 128)) for j in range(8)]
        base = jnp.where(lane_id < 64, 0, 64)
        return [jnp.take_along_axis(X, base + (8*t + j), axis=1) for j in range(8)]

    ahead = [lanes(pair, tiles[0][0], 0) for pair, tiles in groups]
    for t in range(n):
        for g, (pair, A) in enumerate(groups):
            cb = ahead[g]
            P = A[t]
            W = list(P)
            dv = rv = None
            last = t + 1 == n
            if not last:
                X = A[t+1]
                cu = lanes(pair, X[0], t)
                cn = lanes(pair, X[0], t+1)
            others = range(t+2, n)
            if not gj:
                co = {u: lanes(pair, A[u][0], t) for u in others}
            dj = row_of(cb[0], 0)
            for j in range(8):
                r = 1.0 / dj
                dv = dj if j == 0 else jnp.where(sub == j, dj, dv)
                rows = [row_of(p, j) for p in P]
                bs = {i: row_of(cb[j], i) for i in range(j+1, 8)}
                if j < 7:
                    dj = row_of(cb[j+1], j+1) - (bs[j+1] * bs[j+1]) * r
                if gj:
                    rv = r if j == 0 else jnp.where(sub == j, r, rv)
                    mg = jnp.where(sub == j, 0.0, cb[j] * r)
                    W = [w - mg * x for w, x in zip(W, rows)]
                    mf = jnp.where(sub > j, mg, 0.0)
                else:
                    mg = mf = jnp.where(sub > j, cb[j] * r, 0.0)
                P = [p - mf * x for p, x in zip(P, rows)]
                for i in range(j+1, 8):
                    cb[i] = cb[i] - mg * bs[i]
                if not last:
                    m = cu[j] * r
                    X = [a - m * x for a, x in zip(X, rows)]
                    for i in range(8):
                        cn[i] = cn[i] - m * row_of(cu[j], i)
                    for i in range(j+1, 8):
                        cu[i] = cu[i] - m * bs[i]
                if not gj:
                    for u in others:
                        m = co[u][j] * r
                        A[u] = [a - m * x for a, x in zip(A[u], rows)]
                        for i in range(j+1, 8):
                            co[u][i] = co[u][i] - m * bs[i]
            s = lax.rsqrt(dv)
            A[t] = [p * s for p in P]
            if not last:
                A[t+1] = X
                ahead[g] = cn
            if gj and t + 2 < n:
                wr = [[row_of(w * rv, j) for j in range(8)] for w in W]
                for u in others:
                    co = lanes(pair, A[u][0], t)
                    new = []
                    for a, wv in zip(A[u], wr):
                        p = [co[j] * wv[j] for j in range(8)]
                        new.append(a - (((p[0] + p[1]) + (p[2] + p[3])) + ((p[4] + p[5]) + (p[6] + p[7]))))
                    A[u] = new
    return groups


def iotas(rows):
    return lax.broadcasted_iota(jnp.int32, (rows, 128), 0), lax.broadcasted_iota(jnp.int32, (rows, 128), 1)


def rows_of_tiles(*arrays):
    return [[a[8*t:8*t+8, :] for a in arrays] for t in range(8)]


def joined(tiles, i):
    return jnp.concatenate([t[i] for t in tiles], axis=0)


def pair(s):
    row, col = iotas(s.shape[0])
    eye = jnp.where((col == row) | (col == row + 64), 1.0, 0.0)
    return True, [[s[8*t:8*t+8, :], eye[8*t:8*t+8, :]] for t in range(s.shape[0] // 8)]


def inverse(group):
    a = joined(group[1], 1)
    if a.shape[0] < 64:
        a = jnp.concatenate([a, jnp.zeros((64 - a.shape[0], 128), jnp.float32)], axis=0)
    row, col = iotas(128)
    return jnp.where((row < 64) == (col < 64), jnp.concatenate([a, a], axis=0), 0.0)


def sum_and_factor(c_ref, next_hbm, r_ref, rm_ref, v_ref, flat_ref, w_ref, m_ref, acc, r1, s1, r2, r4, res, *more):
    a_refs = more[:6]
    in_sem, pair_send, pair_recv, plane_send, plane_recv, row_recv, line_send, line_recv = more[6:]
    wide, y = lax.axis_index("wide"), lax.axis_index("narrow")
    core, z, x = lax.rem(wide, 2), lax.rem(wide // 2, 8), wide // 16

    def place(x, y, z, core):
        return ((x * 8 + z) * 2 + core, y)

    def in_plane(d):
        return lax.rem(x + d // 8, 4), lax.rem(z + lax.rem(d, 8), 8)

    sibling = place(x, y, z, 1 - core)
    along_y = [place(x, lax.rem(y + d, 8), z, core) for d in range(1, 8)]

    load_w = pltpu.make_async_copy(next_hbm, w_ref, in_sem)
    load_w.start()
    barrier = pltpu.get_barrier_semaphore()
    for other in [sibling] + along_y:
        pl.semaphore_signal(barrier, inc=1, device_id=other, device_id_type=MESH)

    def greet(d, _):
        px, pz = in_plane(d)
        pl.semaphore_signal(barrier, inc=1, device_id=place(px, y, pz, core), device_id_type=MESH)
        return 0

    lax.fori_loop(1, 32, greet, 0)

    def remote(src, dst, send, recv, other):
        return pltpu.make_async_remote_copy(src_ref=src, dst_ref=dst, send_sem=send, recv_sem=recv, device_id=other, device_id_type=MESH)

    def fill(k, a):
        for b, (i, j) in enumerate(PAIRS):
            acc[k, 32*b:32*b+32] = a[128*i:128*i+128, 128*j:128*j+128].reshape(32, 4, 128)

    def whole(ref, send, recv):
        return remote(ref, ref, send, recv, sibling)

    def pair_out(k):
        return remote(acc.at[k, pl.ds(96 * (1 - core), 96)], r1.at[k], pair_send.at[k, 4], pair_recv.at[k, 4], sibling)

    at = 96 * core + 3 * (x * 8 + z)

    def plane_copies(make):
        for dx in (2, 1, 3, 0):
            def step(i, _, dx=dx):
                dz = 1 + lax.rem(2 + i, 7) if dx == 0 else lax.rem(4 + i, 8)
                make(dx, dz, lax.rem(x + dx, 4), lax.rem(z + dz, 8))
                return 0

            lax.fori_loop(1 if dx == 0 else 0, 8, step, 0, unroll=True)

    def plane_out(k):
        def make(dx, dz, px, pz):
            remote(s1.at[k, pl.ds(3 * (px * 8 + pz), 3)], r2.at[k, dx * 8 + dz - 1], plane_send.at[0, k], plane_recv.at[k],
                   place(px, y, pz, core)).start()

        plane_copies(make)

    def plane_back(k):
        mine = res.at[k, pl.ds(at, 3)]

        def make(dx, dz, px, pz):
            remote(mine, mine, plane_send.at[1, k], row_recv.at[k, dx], place(px, y, pz, core)).start()

        plane_copies(make)

    def line(k, d):
        return remote(r4.at[k, y], r4.at[k, y], line_send.at[k, d - 1], line_recv.at[k, d - 1], along_y[d - 1])

    def pair_sum(k):
        pair_out(k).wait_recv()
        s1[k] = acc[k, pl.ds(96 * core, 96)] + r1[k]
        plane_out(k)

    def plane_sum(k):
        whole(r2.at[k], plane_send.at[0, k], plane_recv.at[k]).wait_recv()
        total = s1[k, pl.ds(3 * (x * 8 + z), 3)]
        parts = [r2[k, d] for d in range(31)]
        while len(parts) > 1:
            parts = [a + b for a, b in zip(parts[::2], parts[1::2])] + ([parts[-1]] if len(parts) % 2 else [])
        r4[k, y] = total + parts[0]
        for d in (4, 3, 5, 2, 6, 1, 7):
            line(k, d).start()

    def line_sum(k):
        for d in range(1, 8):
            line(k, d).wait_recv()
        p = [r4[k, d] for d in range(8)]
        res[k, pl.ds(at, 3)] = ((p[0] + p[1]) + (p[2] + p[3])) + ((p[4] + p[5]) + (p[6] + p[7]))
        plane_back(k)

    def pair_back(k, dx):
        row = res.at[k, pl.ds(96 * core + 24 * lax.rem(x + 4 - dx, 4), 24)]
        return remote(row, row, pair_send.at[k, dx], pair_recv.at[k, dx], sibling)

    def gathered(k):
        for dx in (0, 1, 3, 2):
            rows = 21 if dx == 0 else 24
            whole(acc.at[k, pl.ds(0, rows)], plane_send.at[1, k], row_recv.at[k, dx]).wait_recv()
            pair_back(k, dx).start()

    def sent(k):
        pair_out(k).wait_send()
        whole(r2.at[k], plane_send.at[0, k], plane_recv.at[k]).wait_send()
        for d in range(1, 8):
            line(k, d).wait_send()

    def all_back(k):
        for dx in range(4):
            pair_back(k, dx).wait_recv()

    def gram_part(h):
        c = split(c_ref[0])
        wide = slice(128 * h, RANK)
        rows = slice(0, 128) if h == 0 else wide
        a = dot3(tuple(q[:, rows] for q in c), tuple(q[:, wide] for q in c), TN)
        for b, (i, j) in enumerate(PAIRS):
            if (i > 0) == (h > 0):
                i, j = i - h, j - h
                acc[0, 32*b:32*b+32] = a[128*i:128*i+128, 128*j:128*j+128].reshape(32, 4, 128)

    pl.when(core == 1)(lambda: gram_part(0))
    pl.when(core == 0)(lambda: gram_part(1))
    pl.semaphore_wait(barrier, 39)
    pair_out(0).start()
    pl.when(core == 1)(lambda: gram_part(1))
    pl.when(core == 0)(lambda: gram_part(0))
    pair_sum(0)
    load_w.wait()
    w = w_ref[:, 0, :]
    flat_ref[...] = w
    w = split(w)
    fill(1, dot3(w, w, NT))
    pair_out(1).start()
    v_ref[...] = jnp.zeros_like(v_ref)
    r_ref[...] = jnp.zeros_like(r_ref)
    pair_sum(1)
    plane_sum(0)
    plane_sum(1)
    line_sum(0)
    line_sum(1)
    gathered(0)
    sent(0)
    sent(1)
    all_back(0)

    def block(k, b):
        return res[k, 32*b:32*b+32].reshape(128, 128)

    for b, (i, j) in enumerate(PAIRS):
        a = block(0, b)
        a_refs[2*i][:, 128*j:128*j+128] = a[:64]
        a_refs[2*i+1][:, 128*j:128*j+128] = a[64:]
    row, col = iotas(64)
    eye = jnp.where(col == row, 1.0, 0.0)
    for p in range(6):
        o = 128 * (p // 2)
        here = a_refs[p][:, o:o+128]
        if p % 2 == 0:
            ((_, tiles),) = factor([(0, rows_of_tiles(here, eye))], False)
            own = joined(tiles, 1)
            li = own[:, :64]
            near = joined(tiles, 0)
            near = jnp.where((col >= 64) | (col >= row), near, 0.0)
            r_ref[64*p:64*p+64, o:o+128] = near
            rp = near
            a_refs[p+1][:, o:o+128] -= dot3(near[:, 64:], near, TN)
            far = o + 128
        else:
            more_tiles = [a_refs[p][:, o+128:o+256]] if p < 5 else []
            ((_, tiles),) = factor([(64, rows_of_tiles(jnp.where(col >= 64, here, eye), *more_tiles))], False)
            first_tile = joined(tiles, 0)
            li = first_tile[:, :64]
            own = pltpu.roll(jnp.where(col < 64, first_tile, 0.0), 64, 1)
            r_ref[64*p:64*p+64, o:o+128] = jnp.where(col - 64 >= row, first_tile, 0.0)
            rp = jnp.where(col - 64 >= row, first_tile, 0.0)
            if p < 5:
                near = joined(tiles, 1)
                r_ref[64*p:64*p+64, o+128:o+256] = near
                rp = jnp.concatenate([rp, near], axis=1)
                a_refs[p+1][:, o+128:o+256] -= dot3(near[:, :64], near, TN)
            far = o + 256
        if far < RANK:
            rest = dot3(li, a_refs[p][:, far:], NN)
            r_ref[64*p:64*p+64, far:] = rest
            rp = jnp.concatenate([rp, rest], axis=1)
        for q in range(p + 1, 6):
            oq = 128 * (q // 2)
            lq = rp[:, 64*q-o:64*q-o+64]
            if q == p + 1:
                oq += 128
            if oq < RANK:
                a_refs[q][:, oq:] -= dot3(lq, rp[:, oq-o:], TN)
        if p:
            earlier = dot3(r_ref[:64*p, 64*p:64*p+64], v_ref[:64*p, :o+128], TN)
            v_ref[64*p:64*p+64, :o+128] = -dot3(li, earlier, NN)
        v_ref[64*p:64*p+64, o:o+128] += own
        if p == 1:
            gathered(1)
        if p == 3:
            all_back(1)
            for b, (i, j) in enumerate(PAIRS):
                a = block(1, b)
                m_ref[128*i:128*i+128, 128*j:128*j+128] = a
                if i < j:
                    m_ref[128*j:128*j+128, 128*i:128*i+128] = a.T
            rm_ref[:256, :] = dot3(r_ref[:256, :], m_ref[...], NN)
        if p > 3:
            rm_ref[64*p:64*p+64, :] = dot3(rp, m_ref[o:, :], NN)
    for k in range(2):
        whole(r2.at[k], plane_send.at[1, k], plane_recv.at[k]).wait_send()
        for dx in range(4):
            pair_back(k, dx).wait_send()


def first(core, nxt):
    v = pl.BlockSpec(memory_space=pltpu.VMEM)
    f32 = lambda *s: pltpu.VMEM(s, jnp.float32)
    half = lambda *lead: pltpu.VMEM(lead + (4, 128), jnp.float32)
    sems = pltpu.SemaphoreType.DMA
    square = jax.ShapeDtypeStruct((RANK, RANK), jnp.float32)
    return pl.pallas_call(
        sum_and_factor,
        out_shape=(square,) * 4,
        in_specs=[v, pl.BlockSpec(memory_space=pl.ANY)], out_specs=(v,) * 4,
        scratch_shapes=[f32(RANK, 1, RANK), f32(RANK, RANK), half(2, 192), half(2, 96), half(2, 96), half(2, 31, 3), half(2, 8, 3), half(2, 192)]
        + [f32(64, RANK)] * 6
        + [sems(()), sems((2, 5)), sems((2, 5)), sems((2, 2)), sems((2,)), sems((2, 4)), sems((2, 7)), sems((2, 7))],
        compiler_params=pltpu.CompilerParams(collective_id=0, has_side_effects=True, vmem_limit_bytes=51 * 1024 * 1024),
    )(core, nxt)


def iterate(scale, r_ref, rm_ref, v_ref, w_ref, s_ref, c_ref, co_ref, no_ref):
    rm = rm_ref[...]
    a = dot3(jnp.concatenate([dot3(s_ref[...], rm, NN), rm], axis=0), r_ref[...], NT)
    bond = split(a[192:])
    pad = jnp.zeros((16, RANK), jnp.float32)
    stack = lambda *parts: tuple(jnp.concatenate([q[i] for q in parts], axis=0) for i in range(2))
    left = lambda q: (q[0][:, :RANK], q[1][:, :RANK])
    row, col = iotas(64)
    eyes = jnp.where((col == row) | (col == row + 64), 1.0, 0.0)
    y = [jnp.concatenate([a[48*j:48*j+48], pad], axis=0) for j in range(4)]
    ys = [split(v) for v in y]
    done, basis = {}, [None] * 4
    for w in range(ITERS + 3):
        turn = {j: w - j for j in range(4) if 0 <= w - j < ITERS}
        prev, c, s = {}, {}, {}
        for j, k in turn.items():
            if j == 0:
                s[j] = dot3(ys[j], stack(ys[j], ys[j]), NT)
                continue
            prev[j] = stack(*[done[i, k] for i in range(j)])
            e = dot3(ys[j], stack(left(prev[j]), ys[j], *([ys[j]] if j == 2 else [])), NT)
            c[j] = split(e[:, :64*j])
            s[j] = e[:, -128:] - dot3(c[j], stack(c[j], c[j]), NT)
        pairs = [i for i in (0, 2) if i in turn or i + 1 in turn]
        groups = factor([pair(jnp.where(col < 64, s.get(i, eyes), s.get(i + 1, eyes))[:48]) for i in pairs], False)
        onward = [j for j, k in turn.items() if k < ITERS - 1]
        image = dot3(stack(*[ys[j] for j in onward]), bond, NN) if onward else None
        for i, group in zip(pairs, groups):
            wide = any(j in onward for j in (i, i + 1))
            xs = []
            for j in (i, i + 1):
                if j in onward:
                    at = 64 * onward.index(j)
                    x = jnp.concatenate([y[j], image[at:at+64]], axis=1)
                elif j in turn:
                    x = y[j]
                else:
                    x = jnp.zeros((64, 2 * RANK if wide else RANK), jnp.float32)
                if j in prev:
                    x = x - dot3(c[j], prev[j] if j in onward else left(prev[j]), NN)
                if wide and x.shape[1] == RANK:
                    x = jnp.concatenate([x, jnp.zeros((64, RANK), jnp.float32)], axis=1)
                xs.append(x)
            n = dot3(inverse(group), jnp.concatenate(xs, axis=0), NN)
            for j in (i, i + 1):
                if j not in turn:
                    continue
                own = n[64*(j-i):64*(j-i)+64]
                done[j, turn[j]] = split(own if j in onward else own[:, :RANK])
                if j in onward:
                    y[j] = own[:, RANK:]
                    ys[j] = tuple(q[:, RANK:] for q in done[j, turn[j]])
                else:
                    basis[j] = own[:48, :RANK]
    f = split(jnp.concatenate(basis, axis=0))
    co_ref[...] = scale * dot3(dot3(f, v_ref[...], NN), c_ref[0], NT)
    no_ref[:, 0, :] = dot3(dot3(f, r_ref[...], NN), w_ref[...], NN)


def second(r, rm, v, w, start, core, scale):
    vmem = pl.BlockSpec(memory_space=pltpu.VMEM)
    return pl.pallas_call(
        functools.partial(iterate, scale),
        out_shape=(jax.ShapeDtypeStruct((192, RANK), jnp.float32), jax.ShapeDtypeStruct((192, 1, RANK), jnp.float32)),
        in_specs=[vmem] * 6, out_specs=(vmem, vmem),
        compiler_params=pltpu.CompilerParams(vmem_limit_bytes=40 * 1024 * 1024),
    )(r, rm, v, w, start, core)


def shards(core, next_core, start_block):
    r, rm, v, w = first(core, next_core)
    scale = math.sqrt(core.shape[0] * lax.axis_size("wide") * lax.axis_size("narrow") * core.shape[1])
    core_t, next_out = second(r, rm, v, w, start_block.T, core, scale)
    return core_t.T[None], next_out


def solution(mesh):
    placed = (P(("wide", "narrow"), None, None), P(None, ("wide", "narrow"), None), P())
    return jax.shard_map(
        shards,
        mesh=mesh,
        in_specs=placed,
        out_specs=(P(("wide", "narrow"), None, None), P(None, ("wide", "narrow"), None)),
        check_vma=False,
    )
```
